256 devices in a mesh: lat: 32 (over z_hi, x, core), lon: 8 (over y, z_lo).
Axes of the slice: x: 4, y: 4, z: 8 (z_hi: 4, z_lo: 2; z = z_hi * 2 + z_lo), core: 2. Of those that a mesh axis runs over, the one named last changes fastest.
Arguments:
- elevation: float32 [16, 2048, 4096], P(None, 'lat', 'lon'), may hold values from -6 to 6
- depth: float32 [2048, 4096], P('lat', 'lon'), may hold values from 0.3 to 3
- friction: float32 [2048, 4096], P('lat', 'lon'), may hold values from 0.05 to 1
- land_mask: int32 [2048, 4096], P('lat', 'lon'), may hold values 0 or 1
- order_map: int32 [128], replicated, may hold values from 0 to 127, each once
- legendre: bfloat16 [128, 2048, 2048], P('lon', 'lat'), may hold values from -0.125 to 0.125
- load: float32 [2048], replicated, may hold values from 0.25 to 4
Outputs:
- elevation_new: float32 [16, 2048, 4096], P(None, 'lat', 'lon')
- sal: float32 [16, 2048, 4096], P(None, 'lat', 'lon')
- friction_new: float32 [2048, 4096], P('lat', 'lon')
The draws below stay inside these ranges and needn't reach their ends.
Inputs may be any that keep to these rules, and one draw needn't show every extreme that they name: `order_map`: each order 0 to 127 stands in exactly one slot. `land_mask`: 1 marks sea and 0 land.
All inputs are finite; a program needn't handle non-finite values. No bound on the sum of `land_mask` on one device may be relied on, other than what follows from the above.
Results may differ from the reference program's by a relative error of at most 0.0037.
Values may be sent and summed in bfloat16 or wider, within the bound.
No kernel may reach another device: no remote copies, remote signals or barrier semaphores. Data moves between devices by JAX's collectives and lax.ppermute only.
A program may use at most 64 MiB of HBM per device.

```python
import math
import jax
import jax.numpy as jnp
from jax import lax

CONSTITUENTS = 8
DEGREES = 2048
SAMPLES = 64
NLAT = 2048
NLON = 4096
ORDERS = 128


def set_ends(array, rng, least, top_value):
    spot = [jax.random.randint(jax.random.fold_in(rng, axis), (), 0, length) for axis, length in enumerate(array.shape)]
    widest = array.shape.index(max(array.shape))
    neighbour = spot[:widest] + [(spot[widest] + 1) % array.shape[widest]] + spot[widest + 1:]
    return array.at[tuple(spot)].set(least).at[tuple(neighbour)].set(top_value)


def block_levels(stream_key, extent, pieces, smallest, largest):
    level, own = 1.0, jax.random.fold_in(stream_key, 6)
    for axis_at, blocks in pieces:
        steps = jnp.exp(jax.random.uniform(jax.random.fold_in(own, axis_at), (blocks,), jnp.float32, smallest / len(pieces), largest / len(pieces)))
        level = level * jnp.repeat(steps, extent[axis_at] // blocks).reshape([-1 if axis == axis_at else 1 for axis in range(len(extent))])
    return level


def normal_values(rng, shape, scale, limit, shards=(), kind=jnp.bfloat16):
    loudness = block_levels(rng, shape, shards, -0.22, 0.18) if shards else 1.0
    entries = jax.random.normal(rng, shape, jnp.float32) * scale * loudness
    return jnp.minimum(jnp.maximum(entries, -limit), limit).astype(kind)


def setup_inputs(seed: int = 0) -> dict:
    streams_of = jax.random.split(jax.random.key(seed), 8)
    return {
        "elevation": normal_values(streams_of[0], (2 * CONSTITUENTS, NLAT, NLON), 1.0, 6.0, ((1, 32), (2, 8)), jnp.float32),
        "depth": jnp.clip(jnp.exp(math.log(3.0) - 2.3025851 * jax.random.uniform(streams_of[1], (NLAT, NLON), jnp.float32) ** block_levels(streams_of[1], (NLAT, NLON), ((0, 32), (1, 8)), -0.2, 0.2)), 0.3, 3.0),
        "friction": jnp.clip(jnp.exp(math.log(1.0) - 2.9957323 * jax.random.uniform(streams_of[2], (NLAT, NLON), jnp.float32) ** block_levels(streams_of[2], (NLAT, NLON), ((0, 32), (1, 8)), -0.2, 0.2)), 0.05, 1.0),
        "land_mask": set_ends((jax.random.randint(streams_of[3], (NLAT, NLON), 0, 5) < 4).astype(jnp.int32), jax.random.fold_in(streams_of[3], 1), 0, 1),
        "order_map": jax.random.permutation(streams_of[4], ORDERS).astype(jnp.int32),
        "legendre": normal_values(streams_of[5], (ORDERS, NLAT, DEGREES), NLAT ** -0.5, 0.125, ((0, 8), (1, 32))),
        "load": jnp.clip(jnp.exp(jax.random.uniform(streams_of[6], (DEGREES,), jnp.float32, math.log(0.25), math.log(4.0))), 0.25, 4.0),
    }


FREQUENCIES = (1.0, 1.0347, 0.9582, 1.0379, 0.5018, 0.4651, 0.4986, 0.4482)
EQ_AMPS = (0.73, 0.34, 0.14, 0.09, 0.42, 0.3, 0.14, 0.06)
LAT_EDGE = 1.3614
RELAX_RATE = 0.1
BASE_FRICTION = 0.05
DRAG_COEFF = 0.5
SPEED_EPS = 0.001
STEP_TIME = 3.0
PRECISE = lax.Precision.HIGHEST

def fourier_basis(order_map, col_start, lon_cols, lon_count):
    columns = col_start + jnp.arange(lon_cols, dtype=jnp.int32)
    product = order_map[:, None] * columns[None, :] % lon_count
    angles = product.astype(jnp.float32) * (2.0 * math.pi / lon_count)
    scaling = jnp.where(order_map > 0, math.sqrt(2.0 / lon_count), math.sqrt(1.0 / lon_count)).astype(jnp.float32)[:, None]
    harmonics = jnp.stack([jnp.cos(angles) * scaling, jnp.sin(angles) * scaling], axis=1)
    return harmonics.reshape(2 * order_map.shape[0], lon_cols)

def equilibrium(lat_start, lat_rows, col_start, lon_cols, lat_count, lon_count):
    lat_step = 2.0 * LAT_EDGE / lat_count
    lat_offset = jnp.asarray(lat_start).astype(jnp.float32)
    latitude = (-LAT_EDGE + (lat_offset + jnp.arange(lat_rows, dtype=jnp.float32) + 0.5) * lat_step)[:, None]
    columns = jnp.asarray(col_start).astype(jnp.float32) + jnp.arange(lon_cols, dtype=jnp.float32)
    longitude = (columns * (2.0 * math.pi / lon_count))[None, :]
    fields = []
    for member in range(len(EQ_AMPS)):
        if member < 4:
            shape_lat = EQ_AMPS[member] * jnp.cos(latitude) ** 2
            wave_angle = 2.0 * longitude
        else:
            shape_lat = EQ_AMPS[member] * jnp.sin(2.0 * latitude)
            wave_angle = longitude
        fields.append(shape_lat * jnp.cos(wave_angle))
        fields.append(shape_lat * jnp.sin(wave_angle))
    return jnp.stack(fields, axis=0)

def face_flux(depths, drags, diffs, omegas):
    constit = omegas.shape[0]
    pairs = diffs.reshape((constit, 2) + diffs.shape[1:])
    denominator = drags * drags + omegas * omegas * depths * depths
    real_coef = depths * depths * drags / denominator
    imag_coef = depths * depths * depths * omegas / denominator
    flux_real = -(real_coef * pairs[:, 0] - imag_coef * pairs[:, 1])
    flux_imag = -(real_coef * pairs[:, 1] + imag_coef * pairs[:, 0])
    return jnp.stack([flux_real, flux_imag], axis=1).reshape(diffs.shape)

def relax_sweep(padded, elevation, sea_mask, lat_start, lat_count):
    channels, lat_rows, lon_cols = elevation.shape
    surface = padded[:channels]
    sea_depth = padded[channels]
    drag_field = padded[channels + 1]
    lat_step = 2.0 * LAT_EDGE / lat_count
    lat_offset = jnp.asarray(lat_start).astype(jnp.float32)
    cos_center = jnp.cos(-LAT_EDGE + (lat_offset + jnp.arange(lat_rows, dtype=jnp.float32) + 0.5) * lat_step)[:, None]
    cos_face = jnp.cos(-LAT_EDGE + (lat_offset + jnp.arange(lat_rows + 1, dtype=jnp.float32)) * lat_step)[:, None]
    omegas = jnp.asarray(FREQUENCIES, dtype=jnp.float32)[:, None, None]
    east_depth = jnp.sqrt(sea_depth[1:-1, :-1] * sea_depth[1:-1, 1:])
    east_drag = 0.5 * (drag_field[1:-1, :-1] + drag_field[1:-1, 1:])
    east_diff = (surface[:, 1:-1, 1:] - surface[:, 1:-1, :-1]) / cos_center
    north_depth = jnp.sqrt(sea_depth[:-1, 1:-1] * sea_depth[1:, 1:-1])
    north_drag = 0.5 * (drag_field[:-1, 1:-1] + drag_field[1:, 1:-1])
    north_diff = (surface[:, 1:, 1:-1] - surface[:, :-1, 1:-1]) * cos_face
    east_flux = face_flux(east_depth, east_drag, east_diff, omegas)
    north_flux = face_flux(north_depth, north_drag, north_diff, omegas)
    divergence = (east_flux[:, :, 1:] - east_flux[:, :, :-1] + north_flux[:, 1:] - north_flux[:, :-1]) / cos_center
    constit = omegas.shape[0]
    current = elevation.reshape(constit, 2, lat_rows, lon_cols)
    div_pairs = divergence.reshape(constit, 2, lat_rows, lon_cols)
    resid_real = div_pairs[:, 0] + omegas * current[:, 1]
    resid_imag = div_pairs[:, 1] - omegas * current[:, 0]
    residual = jnp.stack([resid_real, resid_imag], axis=1).reshape(channels, lat_rows, lon_cols)
    elevation_new = (elevation - RELAX_RATE * residual) * sea_mask
    east_cell = 0.5 * (east_flux[:, :, 1:] + east_flux[:, :, :-1])
    north_cell = 0.5 * (north_flux[:, 1:] + north_flux[:, :-1])
    return (elevation_new, east_cell, north_cell)

def sample_table():
    sample_time = STEP_TIME * jnp.arange(SAMPLES, dtype=jnp.float32)[:, None]
    omegas = jnp.asarray(FREQUENCIES, dtype=jnp.float32)[None, :]
    phases = sample_time * omegas
    return jnp.stack([jnp.cos(phases), jnp.sin(phases)], axis=2).reshape(SAMPLES, 2 * len(FREQUENCIES))

def reference(elevation, depth, friction, land_mask, order_map, legendre, load):
    channels, lat_count, lon_count = elevation.shape
    slot_count = order_map.shape[0]
    sea_mask = land_mask.astype(jnp.float32)
    masked = (elevation * sea_mask).reshape(channels * lat_count, lon_count)
    harmonics = fourier_basis(order_map, 0, lon_count, lon_count)
    fourier = lax.dot_general(harmonics, masked, (((1,), (1,)), ((), ())), precision=PRECISE, preferred_element_type=jnp.float32)
    fourier = fourier.reshape(slot_count, 2 * channels, lat_count).astype(jnp.bfloat16)

    def one_order(pair):
        tables, values = pair
        coeffs = jnp.dot(values, tables, preferred_element_type=jnp.float32)
        scaled = (coeffs * load[None, :]).astype(jnp.bfloat16)
        return lax.dot_general(scaled, tables, (((1,), (1,)), ((), ())), preferred_element_type=jnp.float32)
    synthesis = lax.map(one_order, (legendre, fourier))
    left_side = synthesis.reshape(2 * slot_count, channels * lat_count)
    sal = lax.dot_general(left_side, harmonics, (((0,), (0,)), ((), ())), precision=PRECISE, preferred_element_type=jnp.float32)
    sal = sal.reshape(channels, lat_count, lon_count)
    equil_tide = equilibrium(0, lat_count, 0, lon_count, lat_count, lon_count)
    surface = elevation - equil_tide - sal
    stacked = jnp.concatenate([surface, (depth * sea_mask)[None], friction[None]], axis=0)
    padded = jnp.pad(stacked, ((0, 0), (1, 1), (0, 0)))
    padded = jnp.concatenate([padded[:, :, -1:], padded, padded[:, :, :1]], axis=2)
    elevation_new, east_cell, north_cell = relax_sweep(padded, elevation, sea_mask, 0, lat_count)
    weights_all = sample_table()

    def add_sample(summed, weights_row):
        east_time = jnp.einsum('c,cjl->jl', weights_row, east_cell, precision=PRECISE)
        north_time = jnp.einsum('c,cjl->jl', weights_row, north_cell, precision=PRECISE)
        speeds = jnp.sqrt(east_time * east_time + north_time * north_time + SPEED_EPS * SPEED_EPS)
        return (summed + speeds, None)
    summed, unused = lax.scan(add_sample, jnp.zeros((lat_count, lon_count), jnp.float32), weights_all)
    friction_new = BASE_FRICTION + DRAG_COEFF * summed / SAMPLES
    return (elevation_new, sal, friction_new)
```

```python
import functools
import math

import jax
import jax.numpy as jnp
import numpy as np
from jax import lax
from jax.experimental import pallas as pl
from jax.experimental.pallas import tpu as pltpu
from jax.sharding import Mesh, PartitionSpec as P

SAMPLES = 64
FREQUENCIES = (1.0, 1.0347, 0.9582, 1.0379, 0.5018, 0.4651, 0.4986, 0.4482)
EQ_AMPS = (0.73, 0.34, 0.14, 0.09, 0.42, 0.3, 0.14, 0.06)
LAT_EDGE = 1.3614
RELAX_RATE = 0.1
BASE_FRICTION = 0.05
DRAG_COEFF = 0.5
SPEED_EPS = 0.001
STEP_TIME = 3.0
NLAT = 2048
NLON = 4096
LAT_STEP = 2.0 * LAT_EDGE / NLAT
ROWS = 64
COLS = 512
CH = 16
DEG = 2048
F32 = jnp.float32
BF16 = jnp.bfloat16
VMEM_LIMIT = 52 * 1024 * 1024


def params():
    return pltpu.CompilerParams(vmem_limit_bytes=VMEM_LIMIT)


def unit_circle(k):
    k = k & (NLON - 1)
    quad = (k + 512) >> 10
    t = (k - (quad << 10)).astype(F32) * (2.0 * math.pi / NLON)
    q = quad & 3
    t2 = t * t
    s = t * (1.0 + t2 * (-1.0 / 6 + t2 * (1.0 / 120 + t2 * (-1.0 / 5040 + t2 * (1.0 / 362880)))))
    c = 1.0 + t2 * (-0.5 + t2 * (1.0 / 24 + t2 * (-1.0 / 720 + t2 * (1.0 / 40320))))
    swap = (q & 1) == 1
    cos = jnp.where(swap, s, c)
    sin = jnp.where(swap, c, s)
    cos = jnp.where((q == 1) | (q == 2), -cos, cos)
    sin = jnp.where(q >= 2, -sin, sin)
    return cos, sin


def split(x):
    hi = x.astype(BF16)
    lo = (x - hi.astype(F32)).astype(BF16)
    return hi, lo


NT = (((1,), (1,)), ((), ()))
TN = (((0,), (0,)), ((), ()))


def dft_kernel(idx, om_ref, elev_ref, mask_ref, part_ref, harm_ref):
    @pl.when(pl.program_id(0) == 0)
    def _():
        lane = lax.broadcasted_iota(jnp.int32, (8, COLS + 128), 1)
        off = jnp.where(lane < COLS, lane, jnp.where(lane < COLS + 64, -1, COLS))
        col = idx[1] * COLS + off
        for g in range(16):
            m = om_ref[8 * g : 8 * g + 8, :]
            cos, sin = unit_circle(m * col)
            scale = jnp.where(m > 0, math.sqrt(2.0 / NLON), math.sqrt(1.0 / NLON)).astype(F32)
            hi, lo = split(jnp.concatenate([cos * scale, sin * scale], axis=0))
            harm_ref[16 * g : 16 * g + 16, :] = hi
            harm_ref[256 + 16 * g : 256 + 16 * g + 16, :] = lo

    mask = mask_ref[...].astype(F32)
    field = jnp.concatenate([elev_ref[c] * mask for c in range(4)], axis=0)
    hi, lo = split(field)
    both = lax.dot_general(harm_ref[:, :COLS], hi, NT, preferred_element_type=F32)
    small = lax.dot_general(harm_ref[:256, :COLS], lo, NT, preferred_element_type=F32)
    out = both[:256] + (both[256:] + small)
    part_ref[...] = out.reshape(16, 16, 256).astype(part_ref.dtype)


def dft(idx, om, elevation, mask, dtype):
    return pl.pallas_call(
        dft_kernel,
        grid_spec=pltpu.PrefetchScalarGridSpec(
            num_scalar_prefetch=1,
            grid=(4,),
            in_specs=[
                pl.BlockSpec((128, 1), lambda i, x: (0, 0)),
                pl.BlockSpec((4, ROWS, COLS), lambda i, x: (i, 0, 0)),
                pl.BlockSpec((ROWS, COLS), lambda i, x: (0, 0)),
            ],
            out_specs=[
                pl.BlockSpec((16, 16, 256), lambda i, x: (0, 0, i)),
                pl.BlockSpec((512, COLS + 128), lambda i, x: (0, 0)),
            ],
        ),
        out_shape=[
            jax.ShapeDtypeStruct((16, 16, 1024), dtype),
            jax.ShapeDtypeStruct((512, COLS + 128), BF16),
        ],
        compiler_params=params(),
        name="dft",
    )(idx, om, elevation, mask)


def analyse_kernel(idx, r_ref, own_ref, rcv_ref, out_ref, a_ref):
    @pl.when(pl.program_id(0) == 0)
    def _():
        me = idx[2]
        lane = lax.broadcasted_iota(jnp.int32, (16, 128), 1)
        low = lane < 64
        for t in range(8):
            tiles = []
            for which in (me, 1 - me):
                acc = r_ref[which, :, 128 * t : 128 * t + 128].astype(F32)
                for d in range(1, 8):
                    acc = acc + r_ref[2 * d + which, :, 128 * t : 128 * t + 128].astype(F32)
                tiles.append(acc)
            f0, f1 = tiles
            even = jnp.where(low, f0, pltpu.roll(f1, 64, 1))
            odd = jnp.where(low, pltpu.roll(f0, 64, 1), f1)
            for ch, val in ((2 * t, even), (2 * t + 1, odd)):
                for p in range(2):
                    for s in range(8):
                        a_ref[s, 16 * p + ch : 16 * p + ch + 1, :] = val[8 * p + s : 8 * p + s + 1, :]

    i = pl.program_id(0)
    for s in range(2):
        a = a_ref[2 * i + s].astype(BF16)
        table = jnp.concatenate([own_ref[s], rcv_ref[s]], axis=0)
        out_ref[s] = jnp.dot(a, table, preferred_element_type=F32).astype(out_ref.dtype)


def analyse(idx, received, legendre, swapped, dtype):
    return pl.pallas_call(
        analyse_kernel,
        grid_spec=pltpu.PrefetchScalarGridSpec(
            num_scalar_prefetch=1,
            grid=(4,),
            in_specs=[
                pl.BlockSpec((16, 16, 1024), lambda i, x: (0, 0, 0)),
                pl.BlockSpec((2, ROWS, DEG), lambda i, x: (4 * x[2] + i, 0, 0)),
                pl.BlockSpec((2, ROWS, DEG), lambda i, x: (i, 0, 0)),
            ],
            out_specs=pl.BlockSpec((2, 32, DEG), lambda i, x: (i, 0, 0)),
            scratch_shapes=[pltpu.VMEM((8, 32, 128), F32)],
        ),
        out_shape=jax.ShapeDtypeStruct((8, 32, DEG), dtype),
        compiler_params=params(),
        name="analyse",
    )(idx, received, legendre, swapped)


def synth_kernel(idx, sc_ref, own_ref, rcv_ref, out_ref, t_ref):
    i = pl.program_id(0)
    for s in range(2):
        table = jnp.concatenate([own_ref[s], rcv_ref[s]], axis=0)
        t_ref[2 * i + s] = lax.dot_general(sc_ref[s], table, NT, preferred_element_type=F32)

    @pl.when(i == 3)
    def _():
        me = idx[2]
        lane = lax.broadcasted_iota(jnp.int32, (8, 128), 1)
        low = lane < 64
        for t in range(8):
            own, oth = [], []
            for p in range(2):
                r0 = 16 * p + 2 * t
                v0 = jnp.concatenate([t_ref[s, r0 : r0 + 1, :] for s in range(8)], axis=0)
                v1 = jnp.concatenate([t_ref[s, r0 + 1 : r0 + 2, :] for s in range(8)], axis=0)
                own.append(jnp.where(low, v0, pltpu.roll(v1, 64, 1)))
                oth.append(jnp.where(low, pltpu.roll(v0, 64, 1), v1))
            own = jnp.concatenate(own, axis=0).astype(out_ref.dtype)
            oth = jnp.concatenate(oth, axis=0).astype(out_ref.dtype)
            for d in range(8):
                out_ref[2 * d + me, :, 128 * t : 128 * t + 128] = own
                out_ref[2 * d + 1 - me, :, 128 * t : 128 * t + 128] = oth


def synthesise(idx, scaled, legendre, swapped, dtype):
    return pl.pallas_call(
        synth_kernel,
        grid_spec=pltpu.PrefetchScalarGridSpec(
            num_scalar_prefetch=1,
            grid=(4,),
            in_specs=[
                pl.BlockSpec((2, 32, DEG), lambda i, x: (i, 0, 0)),
                pl.BlockSpec((2, ROWS, DEG), lambda i, x: (4 * x[2] + i, 0, 0)),
                pl.BlockSpec((2, ROWS, DEG), lambda i, x: (i, 0, 0)),
            ],
            out_specs=pl.BlockSpec((16, 16, 1024), lambda i, x: (0, 0, 0)),
            scratch_shapes=[pltpu.VMEM((8, 32, 128), F32)],
        ),
        out_shape=jax.ShapeDtypeStruct((16, 16, 1024), dtype),
        compiler_params=params(),
        name="synthesise",
    )(idx, scaled, legendre, swapped)


def sal_kernel(g_ref, harm_ref, sal_ref, halo_ref):
    g = g_ref[...]
    hi = lax.dot_general(g, harm_ref[:256, :], TN, preferred_element_type=F32)
    lo = lax.dot_general(g, harm_ref[256:, :], TN, preferred_element_type=F32)
    out = hi + lo
    for c in range(4):
        sal_ref[c] = out[64 * c : 64 * c + 64, :COLS]
        halo_ref[c] = out[64 * c : 64 * c + 64, COLS:]


def inverse(g, harm):
    return pl.pallas_call(
        sal_kernel,
        grid=(4,),
        in_specs=[
            pl.BlockSpec((256, 256), lambda i: (0, i)),
            pl.BlockSpec((512, COLS + 128), lambda i: (0, 0)),
        ],
        out_specs=[
            pl.BlockSpec((4, ROWS, COLS), lambda i: (i, 0, 0)),
            pl.BlockSpec((4, ROWS, 128), lambda i: (i, 0, 0)),
        ],
        out_shape=[
            jax.ShapeDtypeStruct((CH, ROWS, COLS), F32),
            jax.ShapeDtypeStruct((CH, ROWS, 128), F32),
        ],
        compiler_params=params(),
        name="inverse",
    )(g, harm)


def lat_of(row):
    return -LAT_EDGE + row * LAT_STEP


def sweep_kernel(
    idx, elev_ref, sal_ref, salh_ref, salr_ref, depth_ref, fric_ref, mask_ref, rows_ref, lonh_ref, w_ref,
    new_ref, fnew_ref, spad, dpad, fpad, nf,
):
    b = pl.program_id(0)
    lat0 = idx[0] * ROWS

    @pl.when(b == 0)
    def _():
        lane = lax.broadcasted_iota(jnp.int32, (8, COLS), 1)
        col = idx[1] * COLS + lane
        c1, s1 = unit_circle(col)
        c2, s2 = unit_circle(2 * col)
        waves = (c2[:1], s2[:1], c1[:1], s1[:1])

        def shapes(first, count):
            row = first.astype(F32) + lax.broadcasted_iota(jnp.int32, (count, COLS), 0).astype(F32)
            phi = lat_of(row + 0.5)
            cosphi = jnp.cos(phi)
            return cosphi * cosphi, jnp.sin(2.0 * phi)

        sq, s2phi = shapes(lat0, ROWS)
        up_sq, up_s2 = shapes(lat0 - 1, 8)
        dn_sq, dn_s2 = shapes(lat0 + ROWS, 8)
        for ch in range(CH):
            k = ch // 2
            wave = waves[(0 if k < 4 else 2) + ch % 2]
            eq = EQ_AMPS[k] * (sq if k < 4 else s2phi) * wave
            spad[ch, 8 : 8 + ROWS, :] = elev_ref[ch] - eq - sal_ref[ch]
            up = EQ_AMPS[k] * (up_sq if k < 4 else up_s2)[:1] * wave
            dn = EQ_AMPS[k] * (dn_sq if k < 4 else dn_s2)[:1] * wave
            spad[ch, 7:8, :] = rows_ref[0, ch : ch + 1, :] - up - salr_ref[0, ch : ch + 1, :]
            spad[ch, 8 + ROWS : 9 + ROWS, :] = rows_ref[1, ch : ch + 1, :] - dn - salr_ref[1, ch : ch + 1, :]
        dpad[8 : 8 + ROWS, :] = depth_ref[...] * mask_ref[...].astype(F32)
        fpad[8 : 8 + ROWS, :] = fric_ref[...]
        top = jnp.where(idx[0] == 0, 0.0, 1.0)
        bottom = jnp.where(idx[0] == 31, 0.0, 1.0)
        dpad[7:8, :] = rows_ref[0, 16:17, :] * top
        dpad[8 + ROWS : 9 + ROWS, :] = rows_ref[1, 16:17, :] * bottom
        fpad[7:8, :] = rows_ref[0, 17:18, :]
        fpad[8 + ROWS : 9 + ROWS, :] = rows_ref[1, 17:18, :]

        for blk in range(9):
            lo = 8 * blk
            row = (lat0 + lo).astype(F32) + lax.broadcasted_iota(jnp.int32, (8, 128), 0).astype(F32)
            cosf = jnp.tile(jnp.cos(lat_of(row)), (1, 4))
            hh = dpad[8 + lo : 16 + lo, :] * dpad[7 + lo : 15 + lo, :]
            h = jnp.sqrt(hh)
            r = 0.5 * (fpad[8 + lo : 16 + lo, :] + fpad[7 + lo : 15 + lo, :])
            for k in range(8):
                om = FREQUENCIES[k]
                inv = -hh / (r * r + (om * om) * hh)
                rc = inv * r * cosf
                ic = inv * h * om * cosf
                dr = spad[2 * k, 8 + lo : 16 + lo, :] - spad[2 * k, 7 + lo : 15 + lo, :]
                di = spad[2 * k + 1, 8 + lo : 16 + lo, :] - spad[2 * k + 1, 7 + lo : 15 + lo, :]
                nf[2 * k, lo : lo + 8, :] = rc * dr - ic * di
                nf[2 * k + 1, lo : lo + 8, :] = rc * di + ic * dr

    base = pl.multiple_of(8 * b, 8)
    own = pl.ds(base + 8, 8)
    row = (lat0 + base).astype(F32) + lax.broadcasted_iota(jnp.int32, (8, 128), 0).astype(F32)
    phi = lat_of(row + 0.5)
    rcos1 = 1.0 / jnp.cos(phi)
    rcos = jnp.tile(rcos1, (1, 4))
    lane = lax.broadcasted_iota(jnp.int32, (8, COLS), 1)
    last = lane == COLS - 1
    first = lane == 0
    tile_lane = lax.broadcasted_iota(jnp.int32, (8, 128), 1)
    col = idx[1] * COLS + jnp.where(tile_lane < 64, -1, COLS)
    c1, s1 = unit_circle(col)
    c2, s2 = unit_circle(2 * col)
    waves = (c2, s2, c1, s1)
    cosphi = jnp.cos(phi)
    sq, s2phi = cosphi * cosphi, jnp.sin(2.0 * phi)

    def east_of(x, halo):
        wide = jnp.tile(halo, (1, 4))
        return jnp.where(last, wide, pltpu.roll(x, COLS - 1, 1))

    d = dpad[own, :]
    f = fpad[own, :]
    dh = lonh_ref[16]
    fh = lonh_ref[17]
    hh = d * east_of(d, dh)
    h = jnp.sqrt(hh)
    r = 0.5 * (f + east_of(f, fh))
    hhw = d[:, :128] * dh
    hw = jnp.sqrt(hhw)
    rw = 0.5 * (f[:, :128] + fh)
    mask = mask_ref[pl.ds(base, 8), :].astype(F32)
    ecell, ncell = [], []
    for k in range(8):
        om = FREQUENCIES[k]
        inv = -hh / (r * r + (om * om) * hh)
        rc = inv * r * rcos
        ic = inv * h * om * rcos
        invw = -hhw / (rw * rw + (om * om) * hhw)
        rcw = invw * rw * rcos1
        icw = invw * hw * om * rcos1
        diffs, wdiffs = [], []
        for ch in (2 * k, 2 * k + 1):
            s = spad[ch, own, :]
            eq = EQ_AMPS[k] * (sq if k < 4 else s2phi) * waves[(0 if k < 4 else 2) + ch % 2]
            sh = lonh_ref[ch] - eq - salh_ref[ch]
            diffs.append(east_of(s, sh) - s)
            wdiffs.append(s[:, :128] - sh)
        flux = (rc * diffs[0] - ic * diffs[1], rc * diffs[1] + ic * diffs[0])
        fluxw = (rcw * wdiffs[0] - icw * wdiffs[1], rcw * wdiffs[1] + icw * wdiffs[0])
        div = []
        for p in range(2):
            ch = 2 * k + p
            west = jnp.where(first, jnp.tile(fluxw[p], (1, 4)), pltpu.roll(flux[p], 1, 1))
            south = nf[ch, pl.ds(base, 8), :]
            below = nf[ch, pl.ds(base + 8, 8), :]
            sub = lax.broadcasted_iota(jnp.int32, (8, COLS), 0)
            north = pltpu.roll(jnp.where(sub == 0, below, south), 7, 0)
            div.append((flux[p] - west + (north - south)) * rcos)
            ecell.append(0.5 * (flux[p] + west))
            ncell.append(0.5 * (north + south))
        cr = elev_ref[2 * k, pl.ds(base, 8), :]
        ci = elev_ref[2 * k + 1, pl.ds(base, 8), :]
        new_ref[2 * k] = (cr - RELAX_RATE * (div[0] + om * ci)) * mask
        new_ref[2 * k + 1] = (ci - RELAX_RATE * (div[1] - om * cr)) * mask

    def stacked(parts):
        hi, lo = split(jnp.concatenate(parts, axis=0))
        return jnp.concatenate([hi, lo, hi], axis=0)

    xe, xn = stacked(ecell), stacked(ncell)
    total = jnp.zeros((8, COLS), F32)
    for q in range(4):
        w = w_ref[128 * q : 128 * q + 128, :]
        u = jnp.dot(w, xe, preferred_element_type=F32)
        v = jnp.dot(w, xn, preferred_element_type=F32)
        x = u * u + v * v + SPEED_EPS * SPEED_EPS
        speed = x * lax.rsqrt(x)
        for s in range(16):
            total = total + speed[8 * s : 8 * s + 8, :]
    fnew_ref[...] = BASE_FRICTION + DRAG_COEFF * total / SAMPLES


def sample_matrix():
    time = (STEP_TIME * np.arange(SAMPLES, dtype=np.float32))[:, None]
    phases = time * np.asarray(FREQUENCIES, np.float32)[None, :]
    table = np.stack([np.cos(phases), np.sin(phases)], axis=2).reshape(SAMPLES, CH).astype(np.float32)
    hi = table.astype(jnp.bfloat16)
    lo = (table - hi.astype(np.float32)).astype(jnp.bfloat16)
    eye = np.eye(8, dtype=np.float32)
    wide = [np.kron(x.astype(np.float32), eye) for x in (hi, hi, lo)]
    return jnp.asarray(np.concatenate(wide, axis=1), BF16)


def sweep(idx, elevation, sal, salh, salr, depth, friction, mask, rows, lonh, w):
    def whole(shape):
        return pl.BlockSpec(shape, lambda i, x: (0,) * len(shape))

    return pl.pallas_call(
        sweep_kernel,
        grid_spec=pltpu.PrefetchScalarGridSpec(
            num_scalar_prefetch=1,
            grid=(8,),
            in_specs=[
                whole((CH, ROWS, COLS)),
                whole((CH, ROWS, COLS)),
                pl.BlockSpec((CH, 8, 128), lambda i, x: (0, i, 0)),
                whole((2, CH, COLS)),
                whole((ROWS, COLS)),
                whole((ROWS, COLS)),
                whole((ROWS, COLS)),
                whole((2, 18, COLS)),
                pl.BlockSpec((18, 8, 128), lambda i, x: (0, i, 0)),
                whole((512, 384)),
            ],
            out_specs=[
                pl.BlockSpec((CH, 8, COLS), lambda i, x: (0, i, 0)),
                pl.BlockSpec((8, COLS), lambda i, x: (i, 0)),
            ],
            scratch_shapes=[
                pltpu.VMEM((CH, 80, COLS), F32),
                pltpu.VMEM((80, COLS), F32),
                pltpu.VMEM((80, COLS), F32),
                pltpu.VMEM((CH, 72, COLS), F32),
            ],
        ),
        out_shape=[
            jax.ShapeDtypeStruct((CH, ROWS, COLS), F32),
            jax.ShapeDtypeStruct((ROWS, COLS), F32),
        ],
        compiler_params=params(),
        name="sweep",
    )(idx, elevation, sal, salh, salr, depth, friction, mask, rows, lonh, w)


LAT = ("zh", "x", "c")
LON = ("y", "zl")


def shift(value, axes, size, step):
    return lax.ppermute(value, axes, [(i, (i + step) % size) for i in range(size)])


def swap(x, axis):
    return lax.all_to_all(x, axis, 0, 0, tiled=True)


def on_device(elevation, depth, friction, land_mask, order_map, legendre, load):
    lat = lax.axis_index(LAT)
    lon = lax.axis_index(LON)
    core = lax.axis_index("c")
    idx = jnp.stack([lat, lon, core, core]).astype(jnp.int32)

    sent = lax.dynamic_slice_in_dim(legendre, (1 - core) * 8, 8, axis=0)
    swapped = shift(sent, "c", 2, 1)

    sea_depth = depth * land_mask.astype(F32)
    last_row = jnp.concatenate([elevation[:, -1, :], sea_depth[-1:], friction[-1:]], axis=0)
    first_row = jnp.concatenate([elevation[:, 0, :], sea_depth[:1], friction[:1]], axis=0)
    rows = jnp.stack([shift(last_row, LAT, 32, 1), shift(first_row, LAT, 32, -1)])
    last_col = jnp.concatenate([elevation[:, :, -1], sea_depth[None, :, -1], friction[None, :, -1]], axis=0)
    first_col = jnp.concatenate([elevation[:, :, 0], sea_depth[None, :, 0], friction[None, :, 0]], axis=0)
    west = shift(last_col, LON, 8, 1)
    east = shift(first_col, LON, 8, -1)
    half = jnp.arange(128) < 64
    lonh = jnp.where(half, west[:, :, None], east[:, :, None])

    part, harm = dft(idx, order_map[:, None], elevation, land_mask, F32)
    received = swap(part, ("y", "zl", "c"))
    coeffs = analyse(idx, received, legendre, swapped, BF16)
    by_x = swap(coeffs.reshape(4, 64, DEG), "x")
    sum_x = jnp.sum(by_x.astype(F32), axis=0)
    by_z = swap(sum_x.reshape(4, 16, DEG), "zh")
    total = jnp.sum(by_z.astype(F32), axis=0)
    scaled = (total * load[None, :]).astype(BF16)
    all_z = swap(jnp.broadcast_to(scaled[None], (4, 16, DEG)), "zh")
    all_x = swap(jnp.broadcast_to(all_z.reshape(1, 64, DEG), (4, 64, DEG)), "x")
    spread = synthesise(idx, all_x.reshape(8, 32, DEG), legendre, swapped, BF16)
    g = swap(spread, ("y", "zl", "c"))
    sal, salh = inverse(g.reshape(256, 1024), harm)
    salr = jnp.stack([shift(sal[:, -1, :], LAT, 32, 1), shift(sal[:, 0, :], LAT, 32, -1)])
    new, fnew = sweep(idx, elevation, sal, salh, salr, depth, friction, land_mask, rows, lonh, sample_matrix())
    return new, sal, fnew


def solution(mesh):
    fine = Mesh(mesh.devices.reshape(4, 4, 2, 4, 2), ("zh", "x", "c", "y", "zl"))
    return jax.shard_map(
        on_device,
        mesh=fine,
        in_specs=(
            P(None, LAT, LON),
            P(LAT, LON),
            P(LAT, LON),
            P(LAT, LON),
            P(),
            P(LON, LAT, None),
            P(),
        ),
        out_specs=(P(None, LAT, LON), P(None, LAT, LON), P(LAT, LON)),
        check_vma=False,
    )
```

```python
import functools
import math

import jax
import jax.numpy as jnp
import numpy as np
from jax import lax
from jax.experimental import pallas as pl
from jax.experimental.pallas import tpu as pltpu
from jax.sharding import Mesh, PartitionSpec as P

SAMPLES = 64
FREQUENCIES = (1.0, 1.0347, 0.9582, 1.0379, 0.5018, 0.4651, 0.4986, 0.4482)
EQ_AMPS = (0.73, 0.34, 0.14, 0.09, 0.42, 0.3, 0.14, 0.06)
LAT_EDGE = 1.3614
RELAX_RATE = 0.1
BASE_FRICTION = 0.05
DRAG_COEFF = 0.5
SPEED_EPS = 0.001
STEP_TIME = 3.0
NLAT = 2048
NLON = 4096
LAT_STEP = 2.0 * LAT_EDGE / NLAT
ROWS = 64
COLS = 512
CH = 16
DEG = 2048
F32 = jnp.float32
BF16 = jnp.bfloat16
PART_SCALE = 512.0


def params(mib=52):
    return pltpu.CompilerParams(vmem_limit_bytes=mib * 1024 * 1024)


def unit_circle(k):
    k = k & (NLON - 1)
    quad = (k + 512) >> 10
    t = (k - (quad << 10)).astype(F32) * (2.0 * math.pi / NLON)
    q = quad & 3
    t2 = t * t
    s = t * (1.0 + t2 * (-1.0 / 6 + t2 * (1.0 / 120 + t2 * (-1.0 / 5040 + t2 * (1.0 / 362880)))))
    c = 1.0 + t2 * (-0.5 + t2 * (1.0 / 24 + t2 * (-1.0 / 720 + t2 * (1.0 / 40320))))
    swap = (q & 1) == 1
    cos = jnp.where(swap, s, c)
    sin = jnp.where(swap, c, s)
    cos = jnp.where((q == 1) | (q == 2), -cos, cos)
    sin = jnp.where(q >= 2, -sin, sin)
    return cos, sin


def split(x):
    hi = x.astype(BF16)
    lo = (x - hi.astype(F32)).astype(BF16)
    return hi, lo


NT = (((1,), (1,)), ((), ()))
TN = (((0,), (0,)), ((), ()))


def dft_kernel(
    idx, om_ref, elev_ref, mask_ref, depth_ref, fric_ref, leg_ref,
    part_ref, harm_ref, half_ref, first_ref, last_ref, cols_ref,
):
    i = pl.program_id(0)
    half_ref[...] = leg_ref[...]
    mask = mask_ref[...].astype(F32)
    sub = lax.broadcasted_iota(jnp.int32, (8, 128), 0)
    lane = lax.broadcasted_iota(jnp.int32, (8, 128), 1)
    pick_first = jnp.where((sub == 0) & (lane == 0), 1.0, 0.0).astype(F32)
    pick_last = jnp.where((sub == 1) & (lane == 127), 1.0, 0.0).astype(F32)

    def ends(x):
        def pick(sel, tile):
            return lax.dot_general(sel, tile, NT, precision=lax.Precision.HIGHEST, preferred_element_type=F32)

        return pick(pick_first, x[:, :128]) + pick(pick_last, x[:, COLS - 128 :])

    @pl.when(i == 0)
    def _():
        diag = lax.broadcasted_iota(jnp.int32, (128, 128), 0) == lax.broadcasted_iota(jnp.int32, (128, 128), 1)
        orders = jnp.broadcast_to(om_ref[...].astype(F32), (128, 128))
        orders = jnp.sum(jnp.where(diag, orders, 0.0), axis=1, keepdims=True).astype(jnp.int32)
        lane = lax.broadcasted_iota(jnp.int32, (8, COLS + 128), 1)
        off = jnp.where(lane < COLS, lane, jnp.where(lane < COLS + 64, -1, COLS))
        col = idx[1] * COLS + off
        for g in range(16):
            m = orders[8 * g : 8 * g + 8, :]
            cos, sin = unit_circle(m * col)
            scale = jnp.where(m > 0, math.sqrt(2.0 / NLON), math.sqrt(1.0 / NLON)).astype(F32)
            hi, lo = split(jnp.concatenate([cos * scale, sin * scale], axis=0))
            harm_ref[16 * g : 16 * g + 16, :] = hi
            harm_ref[256 + 16 * g : 256 + 16 * g + 16, :] = lo
        sea = depth_ref[...] * mask
        for r, x in ((16, sea), (17, fric_ref[...])):
            first_ref[r : r + 1, :] = x[:1]
            last_ref[r : r + 1, :] = x[ROWS - 1 :]
        first_ref[18:, :] = jnp.zeros((6, COLS), F32)
        last_ref[18:, :] = jnp.zeros((6, COLS), F32)
        cols_ref[:, 1024:] = ends(jnp.concatenate([sea, fric_ref[...]], axis=0))

    field = jnp.concatenate([elev_ref[c] * mask for c in range(4)], axis=0)
    hi, lo = split(field)
    both = lax.dot_general(harm_ref[:, :COLS], hi, NT, preferred_element_type=F32)
    small = lax.dot_general(harm_ref[:256, :COLS], lo, NT, preferred_element_type=F32)
    out = both[:256] + (both[256:] + small)
    part_ref[...] = (out * PART_SCALE).reshape(16, 16, 256).astype(part_ref.dtype)
    for c in range(4):
        first_ref[pl.ds(4 * i + c, 1), :] = field[64 * c : 64 * c + 1]
        last_ref[pl.ds(4 * i + c, 1), :] = field[64 * c + 63 : 64 * c + 64]
    cols_ref[:, pl.ds(pl.multiple_of(256 * i, 256), 256)] = ends(field)


def dft(idx, om, elevation, mask, depth, friction, legendre):
    def whole(shape):
        return pl.BlockSpec(shape, lambda i, x: (0,) * len(shape))

    return pl.pallas_call(
        dft_kernel,
        grid_spec=pltpu.PrefetchScalarGridSpec(
            num_scalar_prefetch=1,
            grid=(4,),
            in_specs=[
                whole((1, 128)),
                pl.BlockSpec((4, ROWS, COLS), lambda i, x: (i, 0, 0)),
                whole((ROWS, COLS)),
                whole((ROWS, COLS)),
                whole((ROWS, COLS)),
                pl.BlockSpec((2, ROWS, DEG), lambda i, x: (4 - 4 * x[2] + i, 0, 0)),
            ],
            out_specs=[
                pl.BlockSpec((16, 16, 256), lambda i, x: (0, 0, i)),
                whole((512, COLS + 128)),
                pl.BlockSpec((2, ROWS, DEG), lambda i, x: (i, 0, 0)),
                whole((24, COLS)),
                whole((24, COLS)),
                whole((8, 1152)),
            ],
        ),
        out_shape=[
            jax.ShapeDtypeStruct((16, 16, 1024), F32),
            jax.ShapeDtypeStruct((512, COLS + 128), BF16),
            jax.ShapeDtypeStruct((8, ROWS, DEG), BF16),
            jax.ShapeDtypeStruct((24, COLS), F32),
            jax.ShapeDtypeStruct((24, COLS), F32),
            jax.ShapeDtypeStruct((8, 1152), F32),
        ],
        compiler_params=params(60),
        name="dft",
    )(idx, om, elevation, mask, depth, friction, legendre)


def analyse_kernel(idx, r_ref, own_ref, rcv_ref, *rest):
    out_ref, mid_ref, outer_ref, a_ref, e_ref = rest[-5:]

    @pl.when(pl.program_id(0) == 0)
    def _():
        me = idx[2]
        low = lax.broadcasted_iota(jnp.int32, (16, 128), 1) < 64
        for t in range(8):
            tiles = [r_ref[which, :, 128 * t : 128 * t + 128] for which in (me, 1 - me)]
            f0, f1 = tiles
            even = jnp.where(low, f0, pltpu.roll(f1, 64, 1))
            odd = jnp.where(low, pltpu.roll(f0, 64, 1), f1)
            for ch, val in ((2 * t, even), (2 * t + 1, odd)):
                for p in range(2):
                    a_ref[pl.ds(16 * p + ch, 8, stride=32), :] = val[8 * p : 8 * p + 8, :]

    i = pl.program_id(0)
    for s in range(2):
        a = a_ref[pl.ds(pl.multiple_of(64 * i, 64) + 32 * s, 32), :].astype(BF16)
        table = jnp.concatenate([own_ref[s], rcv_ref[s]], axis=0)
        out_ref[s] = jnp.dot(a, table, preferred_element_type=F32).astype(out_ref.dtype)
        low = idx[2] == 0
        own_first, own_last = own_ref[s, :16].astype(F32)[:1], own_ref[s, ROWS - 16 :].astype(F32)[15:]
        rcv_first, rcv_last = rcv_ref[s, :16].astype(F32)[:1], rcv_ref[s, ROWS - 16 :].astype(F32)[15:]
        e_ref[pl.ds(2 * i + s, 1), :] = jnp.where(low, rcv_first, own_first)
        e_ref[pl.ds(8 + 2 * i + s, 1), :] = jnp.where(low, own_last, rcv_last)
        e_ref[pl.ds(16 + 2 * i + s, 1), :] = jnp.where(low, own_first, rcv_first)
        e_ref[pl.ds(24 + 2 * i + s, 1), :] = jnp.where(low, rcv_last, own_last)

    @pl.when(i == 3)
    def _():
        mid_ref[...] = e_ref[:16, :].astype(BF16)
        outer_ref[...] = e_ref[16:, :].astype(BF16)


def analyse(idx, received, legendre, other, after, dtype):
    table = pl.BlockSpec((2, ROWS, DEG), lambda i, x: (4 * x[2] + i, 0, 0))
    return pl.pallas_call(
        analyse_kernel,
        grid_spec=pltpu.PrefetchScalarGridSpec(
            num_scalar_prefetch=1,
            grid=(4,),
            in_specs=[
                pl.BlockSpec((2, 16, 1024), lambda i, x: (0, 0, 0)),
                table,
                pl.BlockSpec((2, ROWS, DEG), lambda i, x: (i, 0, 0)),
            ]
            + [pl.BlockSpec(memory_space=pl.ANY)] * len(after),
            out_specs=[
                pl.BlockSpec((2, 32, DEG), lambda i, x: (i, 0, 0)),
                pl.BlockSpec((16, DEG), lambda i, x: (0, 0)),
                pl.BlockSpec((16, DEG), lambda i, x: (0, 0)),
            ],
            scratch_shapes=[pltpu.VMEM((256, 128), F32), pltpu.VMEM((32, DEG), F32)],
        ),
        out_shape=[
            jax.ShapeDtypeStruct((8, 32, DEG), dtype),
            jax.ShapeDtypeStruct((16, DEG), BF16),
            jax.ShapeDtypeStruct((16, DEG), BF16),
        ],
        compiler_params=params(),
        name="analyse",
    )(idx, received, legendre, other, *after)


def synth_kernel(idx, sc_ref, own_ref, rcv_ref, mid_ref, prev_ref, next_ref, *rest):
    out_ref, t_ref, u_ref = rest[-3:]
    edges = jnp.concatenate([mid_ref[...], prev_ref[...], next_ref[...]], axis=0)
    i = pl.program_id(0)
    for s in range(2):
        table = jnp.concatenate([own_ref[s], rcv_ref[s]], axis=0)
        row = pl.multiple_of(64 * i, 64) + 32 * s
        t_ref[pl.ds(row, 32), :] = lax.dot_general(sc_ref[s], table, NT, preferred_element_type=F32)
        u_ref[2 * i + s, :, :32] = lax.dot_general(edges, sc_ref[s], NT, preferred_element_type=F32)

    @pl.when(i == 3)
    def _():
        me = idx[2]
        lane = lax.broadcasted_iota(jnp.int32, (8, 128), 1)
        sub = lax.broadcasted_iota(jnp.int32, (8, 128), 0)
        low = lane < 64
        for t in range(8):
            own, oth = [], []
            for p in range(2):
                v0 = t_ref[pl.ds(16 * p + 2 * t, 8, stride=32), :]
                v1 = t_ref[pl.ds(16 * p + 2 * t + 1, 8, stride=32), :]
                own.append(jnp.where(low, v0, pltpu.roll(v1, 64, 1)))
                oth.append(jnp.where(low, pltpu.roll(v0, 64, 1), v1))
            own = jnp.concatenate(own, axis=0).astype(out_ref.dtype)
            oth = jnp.concatenate(oth, axis=0).astype(out_ref.dtype)
            for d in range(8):
                out_ref[2 * d + me, :, 128 * t : 128 * t + 128] = own
                out_ref[2 * d + 1 - me, :, 128 * t : 128 * t + 128] = oth
        for half in range(2):
            sides = []
            for side in range(2):
                g = 8 * ((3, 0), (1, 4))[half][side]
                v = jnp.zeros((8, 128), F32)
                for s in range(8):
                    v = jnp.where(sub == s, u_ref[s, g : g + 8, :], v)
                sides.append(v)
            top, bottom = sides
            rows = [
                jnp.where(lane < 16, top, pltpu.roll(bottom, 16, 1)),
                jnp.where(lane < 16, pltpu.roll(top, 112, 1), bottom),
            ]
            rows = [jnp.where(lane < 32, x, 0.0) for x in rows]
            edge = jnp.concatenate(rows, axis=0).astype(out_ref.dtype)
            for d in range(8):
                out_ref[2 * d + half, :, 1024:] = edge


def synthesise(idx, scaled, legendre, other, edges, after, dtype):
    table = pl.BlockSpec((2, ROWS, DEG), lambda i, x: (4 * x[2] + i, 0, 0))
    return pl.pallas_call(
        synth_kernel,
        grid_spec=pltpu.PrefetchScalarGridSpec(
            num_scalar_prefetch=1,
            grid=(4,),
            in_specs=[
                pl.BlockSpec((2, 32, DEG), lambda i, x: (i, 0, 0)),
                table,
                pl.BlockSpec((2, ROWS, DEG), lambda i, x: (i, 0, 0)),
            ]
            + [pl.BlockSpec((16, DEG), lambda i, x: (0, 0))] * 3
            + [pl.BlockSpec(memory_space=pl.ANY)] * len(after),
            out_specs=pl.BlockSpec((16, 16, 1152), lambda i, x: (0, 0, 0)),
            scratch_shapes=[pltpu.VMEM((256, 128), F32), pltpu.VMEM((8, 48, 128), F32)],
        ),
        out_shape=jax.ShapeDtypeStruct((16, 16, 1152), dtype),
        compiler_params=params(),
        name="synthesise",
    )(idx, scaled, legendre, other, *edges, *after)


def lat_of(row):
    return -LAT_EDGE + row * LAT_STEP


def sweep_kernel(
    idx, g_ref, harm_ref, elev_ref, depth_ref, fric_ref, mask_ref, before_ref, after_ref, west_ref, east_ref, w_ref,
    new_ref, sal_ref, fnew_ref, spad, dpad, fpad, nf, salbuf, lonh_all, sem,
):
    b = pl.program_id(0)
    lat0 = idx[0] * ROWS

    def send(c):
        part = pl.ds(4 * c, 4)
        return pltpu.make_async_copy(salbuf.at[part], sal_ref.at[part], sem.at[c])

    @pl.when(b == 0)
    def _():
        lane = lax.broadcasted_iota(jnp.int32, (8, COLS), 1)
        col = idx[1] * COLS + lane
        c1, s1 = unit_circle(col)
        c2, s2 = unit_circle(2 * col)
        waves = (c2[:1], s2[:1], c1[:1], s1[:1])

        def shapes(first, count):
            row = first.astype(F32) + lax.broadcasted_iota(jnp.int32, (count, 128), 0).astype(F32)
            phi = lat_of(row + 0.5)
            cosphi = jnp.cos(phi)
            return jnp.tile(cosphi * cosphi, (1, 4)), jnp.tile(jnp.sin(2.0 * phi), (1, 4))

        sq, s2phi = shapes(lat0, ROWS)
        up_sq, up_s2 = shapes(lat0 - 1, 8)
        dn_sq, dn_s2 = shapes(lat0 + ROWS, 8)

        def invert(cols):
            part = g_ref[:, cols]
            hi = lax.dot_general(part, harm_ref[:256, :], TN, preferred_element_type=F32)
            lo = lax.dot_general(part, harm_ref[256:, :], TN, preferred_element_type=F32)
            return hi + lo

        sub = lax.broadcasted_iota(jnp.int32, (8, 128), 0)
        lane = lax.broadcasted_iota(jnp.int32, (8, 128), 1)
        to_low = jnp.where((sub == 1) & (lane < 64), 1.0, 0.0).astype(F32)
        to_high = jnp.where((sub == 0) & (lane >= 64), 1.0, 0.0).astype(F32)

        def place(x, sel):
            return lax.dot_general(x, sel, TN, precision=lax.Precision.HIGHEST, preferred_element_type=F32)

        beside = place(west_ref[...], to_low) + place(east_ref[...], to_high)
        for ch in range(18):
            lonh_all[ch] = beside[64 * ch : 64 * ch + 64]
        edge = invert(slice(1024, 1152))
        for ch in range(CH):
            if ch % 4 == 0:
                quarter = invert(slice(64 * ch, 64 * ch + 256))
                for c in range(4):
                    salbuf[ch + c] = quarter[64 * c : 64 * c + 64, :COLS]
                    lonh_all[ch + c] = lonh_all[ch + c] - quarter[64 * c : 64 * c + 64, COLS:]
                send(ch // 4).start()
            k = ch // 2
            wave = waves[(0 if k < 4 else 2) + ch % 2]
            eq = EQ_AMPS[k] * (sq if k < 4 else s2phi) * wave
            spad[ch, 8 : 8 + ROWS, :] = elev_ref[ch] - eq - salbuf[ch]
            up = EQ_AMPS[k] * (up_sq if k < 4 else up_s2)[:1] * wave
            dn = EQ_AMPS[k] * (dn_sq if k < 4 else dn_s2)[:1] * wave
            spad[ch, 7:8, :] = before_ref[ch : ch + 1, :] - up - edge[ch : ch + 1, :COLS]
            spad[ch, 8 + ROWS : 9 + ROWS, :] = after_ref[ch : ch + 1, :] - dn - edge[16 + ch : 17 + ch, :COLS]
        dpad[8 : 8 + ROWS, :] = depth_ref[...] * mask_ref[...].astype(F32)
        fpad[8 : 8 + ROWS, :] = fric_ref[...]
        top = jnp.where(idx[0] == 0, 0.0, 1.0)
        bottom = jnp.where(idx[0] == 31, 0.0, 1.0)
        dpad[7:8, :] = before_ref[16:17, :] * top
        dpad[8 + ROWS : 9 + ROWS, :] = after_ref[16:17, :] * bottom
        fpad[7:8, :] = before_ref[17:18, :]
        fpad[8 + ROWS : 9 + ROWS, :] = after_ref[17:18, :]

        for blk in range(9):
            lo = 8 * blk
            row = (lat0 + lo).astype(F32) + lax.broadcasted_iota(jnp.int32, (8, 128), 0).astype(F32)
            cosf = jnp.tile(jnp.cos(lat_of(row)), (1, 4))
            hh = dpad[8 + lo : 16 + lo, :] * dpad[7 + lo : 15 + lo, :]
            h = jnp.sqrt(hh)
            r = 0.5 * (fpad[8 + lo : 16 + lo, :] + fpad[7 + lo : 15 + lo, :])
            for k in range(8):
                om = FREQUENCIES[k]
                inv = -hh / (r * r + (om * om) * hh)
                rc = inv * r * cosf
                ic = inv * h * om * cosf
                dr = spad[2 * k, 8 + lo : 16 + lo, :] - spad[2 * k, 7 + lo : 15 + lo, :]
                di = spad[2 * k + 1, 8 + lo : 16 + lo, :] - spad[2 * k + 1, 7 + lo : 15 + lo, :]
                nf[2 * k, lo : lo + 8, :] = rc * dr - ic * di
                nf[2 * k + 1, lo : lo + 8, :] = rc * di + ic * dr

    base = pl.multiple_of(8 * b, 8)
    own = pl.ds(base + 8, 8)
    row = (lat0 + base).astype(F32) + lax.broadcasted_iota(jnp.int32, (8, 128), 0).astype(F32)
    phi = lat_of(row + 0.5)
    rcos1 = 1.0 / jnp.cos(phi)
    rcos = jnp.tile(rcos1, (1, 4))
    lane = lax.broadcasted_iota(jnp.int32, (8, COLS), 1)
    last = lane == COLS - 1
    first = lane == 0
    tile_lane = lax.broadcasted_iota(jnp.int32, (8, 128), 1)
    col = idx[1] * COLS + jnp.where(tile_lane < 64, -1, COLS)
    c1, s1 = unit_circle(col)
    c2, s2 = unit_circle(2 * col)
    waves = (c2, s2, c1, s1)
    cosphi = jnp.cos(phi)
    sq, s2phi = cosphi * cosphi, jnp.sin(2.0 * phi)

    def east_of(x, halo):
        wide = jnp.tile(halo, (1, 4))
        return jnp.where(last, wide, pltpu.roll(x, COLS - 1, 1))

    d = dpad[own, :]
    f = fpad[own, :]
    dh = lonh_all[16, pl.ds(base, 8), :]
    fh = lonh_all[17, pl.ds(base, 8), :]
    hh = d * east_of(d, dh)
    h = jnp.sqrt(hh)
    r = 0.5 * (f + east_of(f, fh))
    hhw = d[:, :128] * dh
    hw = jnp.sqrt(hhw)
    rw = 0.5 * (f[:, :128] + fh)
    mask = mask_ref[pl.ds(base, 8), :].astype(F32)
    ecell, ncell = [], []
    for k in range(8):
        om = FREQUENCIES[k]
        inv = -hh / (r * r + (om * om) * hh)
        rc = inv * r * rcos
        ic = inv * h * om * rcos
        invw = -hhw / (rw * rw + (om * om) * hhw)
        rcw = invw * rw * rcos1
        icw = invw * hw * om * rcos1
        diffs, wdiffs = [], []
        for ch in (2 * k, 2 * k + 1):
            s = spad[ch, own, :]
            eq = EQ_AMPS[k] * (sq if k < 4 else s2phi) * waves[(0 if k < 4 else 2) + ch % 2]
            sh = lonh_all[ch, pl.ds(base, 8), :] - eq
            diffs.append(east_of(s, sh) - s)
            wdiffs.append(s[:, :128] - sh)
        flux = (rc * diffs[0] - ic * diffs[1], rc * diffs[1] + ic * diffs[0])
        fluxw = (rcw * wdiffs[0] - icw * wdiffs[1], rcw * wdiffs[1] + icw * wdiffs[0])
        div = []
        for p in range(2):
            ch = 2 * k + p
            west = jnp.where(first, jnp.tile(fluxw[p], (1, 4)), pltpu.roll(flux[p], 1, 1))
            south = nf[ch, pl.ds(base, 8), :]
            below = nf[ch, pl.ds(base + 8, 8), :]
            sub = lax.broadcasted_iota(jnp.int32, (8, COLS), 0)
            north = pltpu.roll(jnp.where(sub == 0, below, south), 7, 0)
            div.append((flux[p] - west + (north - south)) * rcos)
            ecell.append(0.5 * (flux[p] + west))
            ncell.append(0.5 * (north + south))
        cr = elev_ref[2 * k, pl.ds(base, 8), :]
        ci = elev_ref[2 * k + 1, pl.ds(base, 8), :]
        new_ref[2 * k] = (cr - RELAX_RATE * (div[0] + om * ci)) * mask
        new_ref[2 * k + 1] = (ci - RELAX_RATE * (div[1] - om * cr)) * mask

    def stacked(parts):
        hi, lo = split(jnp.concatenate(parts, axis=0))
        return jnp.concatenate([hi, lo, hi], axis=0)

    xe, xn = stacked(ecell), stacked(ncell)
    total = jnp.zeros((8, COLS), F32)
    for q in range(4):
        w = w_ref[128 * q : 128 * q + 128, :]
        u = jnp.dot(w, xe, preferred_element_type=F32)
        v = jnp.dot(w, xn, preferred_element_type=F32)
        x = u * u + v * v + SPEED_EPS * SPEED_EPS
        speed = x * lax.rsqrt(x)
        for s in range(16):
            total = total + speed[8 * s : 8 * s + 8, :]
    fnew_ref[...] = BASE_FRICTION + DRAG_COEFF * total / SAMPLES

    @pl.when(b == 7)
    def _():
        for c in range(4):
            send(c).wait()


def sample_matrix():
    time = (STEP_TIME * np.arange(SAMPLES, dtype=np.float32))[:, None]
    phases = time * np.asarray(FREQUENCIES, np.float32)[None, :]
    table = np.stack([np.cos(phases), np.sin(phases)], axis=2).reshape(SAMPLES, CH).astype(np.float32)
    hi = table.astype(jnp.bfloat16)
    lo = (table - hi.astype(np.float32)).astype(jnp.bfloat16)
    eye = np.eye(8, dtype=np.float32)
    wide = [np.kron(x.astype(np.float32), eye) for x in (hi, hi, lo)]
    return jnp.asarray(np.concatenate(wide, axis=1), BF16)


def sweep(idx, g, harm, elevation, depth, friction, mask, before, after, west, east, w):
    def whole(shape):
        return pl.BlockSpec(shape, lambda i, x: (0,) * len(shape))

    return pl.pallas_call(
        sweep_kernel,
        grid_spec=pltpu.PrefetchScalarGridSpec(
            num_scalar_prefetch=1,
            grid=(8,),
            in_specs=[
                whole((256, 1152)),
                whole((512, COLS + 128)),
                whole((CH, ROWS, COLS)),
                whole((ROWS, COLS)),
                whole((ROWS, COLS)),
                whole((ROWS, COLS)),
                whole((24, COLS)),
                whole((24, COLS)),
                whole((8, 1152)),
                whole((8, 1152)),
                whole((512, 384)),
            ],
            out_specs=[
                pl.BlockSpec((CH, 8, COLS), lambda i, x: (0, i, 0)),
                pl.BlockSpec(memory_space=pl.ANY),
                pl.BlockSpec((8, COLS), lambda i, x: (i, 0)),
            ],
            scratch_shapes=[
                pltpu.VMEM((CH, 80, COLS), F32),
                pltpu.VMEM((80, COLS), F32),
                pltpu.VMEM((80, COLS), F32),
                pltpu.VMEM((CH, 72, COLS), F32),
                pltpu.VMEM((CH, ROWS, COLS), F32),
                pltpu.VMEM((CH + 2, ROWS, 128), F32),
                pltpu.SemaphoreType.DMA((4,)),
            ],
        ),
        out_shape=[
            jax.ShapeDtypeStruct((CH, ROWS, COLS), F32),
            jax.ShapeDtypeStruct((CH, ROWS, COLS), F32),
            jax.ShapeDtypeStruct((ROWS, COLS), F32),
        ],
        compiler_params=params(),
        name="sweep",
    )(idx, g, harm, elevation, depth, friction, mask, before, after, west, east, w)


LAT = ("zh", "x", "c")
LON = ("y", "zl")


def shift(value, axes, size, step):
    return lax.ppermute(value, axes, [(i, (i + step) % size) for i in range(size)])


def swap(x, axis):
    return lax.all_to_all(x, axis, 0, 0, tiled=True)


def on_device(elevation, depth, friction, land_mask, order_map, legendre, load):
    lat = lax.axis_index(LAT)
    lon = lax.axis_index(LON)
    core = lax.axis_index("c")
    idx = jnp.stack([lat, lon, core, core]).astype(jnp.int32)

    part, harm, half, first_row, last_row, ends = dft(
        idx, order_map[None, :], elevation, land_mask, depth, friction, legendre
    )
    received = swap(part.astype(jnp.float16), ("y", "zl", "c"))
    other = shift(half, "c", 2, 1)
    before = shift(last_row, LAT, 32, 1)
    after = shift(first_row, LAT, 32, -1)
    west = shift(ends, LON, 8, 1)
    east = shift(ends, LON, 8, -1)
    fourier = jnp.sum(received.reshape(8, 2, 16, 1024).astype(F32), axis=0) * (1.0 / PART_SCALE)
    coeffs, mid, outer = analyse(idx, fourier, legendre, other, (before, after), BF16)
    prior = shift(outer, LAT, 32, 2)
    later = shift(outer, LAT, 32, -2)

    by_band = swap(coeffs.reshape(16, 16, DEG), ("zh", "x"))
    total = jnp.sum(by_band.astype(F32), axis=0)
    scaled = (total * load[None, :]).astype(BF16)
    every = swap(jnp.broadcast_to(scaled[None], (16, 16, DEG)), ("zh", "x"))
    spread = synthesise(idx, every.reshape(8, 32, DEG), legendre, other, (mid, prior, later), (west, east), BF16)
    g = swap(spread, ("y", "zl", "c"))
    new, sal, fnew = sweep(
        idx, g.reshape(256, 1152), harm, elevation, depth, friction, land_mask,
        before, after, west, east, sample_matrix(),
    )
    return new, sal, fnew


def solution(mesh):
    fine = Mesh(mesh.devices.reshape(4, 4, 2, 4, 2), ("zh", "x", "c", "y", "zl"))
    return jax.shard_map(
        on_device,
        mesh=fine,
        in_specs=(
            P(None, LAT, LON),
            P(LAT, LON),
            P(LAT, LON),
            P(LAT, LON),
            P(),
            P(LON, LAT, None),
            P(),
        ),
        out_specs=(P(None, LAT, LON), P(None, LAT, LON), P(LAT, LON)),
        check_vma=False,
    )
```

```python
import functools
import math

import jax
import jax.numpy as jnp
import numpy as np
from jax import lax
from jax.experimental import pallas as pl
from jax.experimental.pallas import tpu as pltpu
from jax.sharding import Mesh, PartitionSpec as P

SAMPLES = 64
FREQUENCIES = (1.0, 1.0347, 0.9582, 1.0379, 0.5018, 0.4651, 0.4986, 0.4482)
EQ_AMPS = (0.73, 0.34, 0.14, 0.09, 0.42, 0.3, 0.14, 0.06)
LAT_EDGE = 1.3614
RELAX_RATE = 0.1
BASE_FRICTION = 0.05
DRAG_COEFF = 0.5
SPEED_EPS = 0.001
STEP_TIME = 3.0
NLAT = 2048
NLON = 4096
LAT_STEP = 2.0 * LAT_EDGE / NLAT
ROWS = 64
COLS = 512
CH = 16
DEG = 2048
F32 = jnp.float32
BF16 = jnp.bfloat16
PART_SCALE = 512.0


def params(mib=24):
    return pltpu.CompilerParams(vmem_limit_bytes=mib * 1024 * 1024)


def unit_circle(k):
    k = k & (NLON - 1)
    quad = (k + 512) >> 10
    t = (k - (quad << 10)).astype(F32) * (2.0 * math.pi / NLON)
    q = quad & 3
    t2 = t * t
    s = t * (1.0 + t2 * (-1.0 / 6 + t2 * (1.0 / 120 + t2 * (-1.0 / 5040 + t2 * (1.0 / 362880)))))
    c = 1.0 + t2 * (-0.5 + t2 * (1.0 / 24 + t2 * (-1.0 / 720 + t2 * (1.0 / 40320))))
    swap = (q & 1) == 1
    cos = jnp.where(swap, s, c)
    sin = jnp.where(swap, c, s)
    cos = jnp.where((q == 1) | (q == 2), -cos, cos)
    sin = jnp.where(q >= 2, -sin, sin)
    return cos, sin


def split(x):
    hi = x.astype(BF16)
    lo = (x - hi.astype(F32)).astype(BF16)
    return hi, lo


NT = (((1,), (1,)), ((), ()))
TN = (((0,), (0,)), ((), ()))


def dft_kernel(
    idx, om_ref, elev_ref, mask_ref, depth_ref, fric_ref, leg_ref,
    part_ref, harm_ref, half_ref, first_ref, last_ref, cols_ref,
):
    i = pl.program_id(0)
    half_ref[...] = leg_ref[...]
    mask = mask_ref[...].astype(F32)
    @pl.when(i == 0)
    def _():
        diag = lax.broadcasted_iota(jnp.int32, (128, 128), 0) == lax.broadcasted_iota(jnp.int32, (128, 128), 1)
        orders = jnp.broadcast_to(om_ref[...].astype(F32), (128, 128))
        orders = jnp.sum(jnp.where(diag, orders, 0.0), axis=1, keepdims=True).astype(jnp.int32)
        lane = lax.broadcasted_iota(jnp.int32, (8, COLS + 128), 1)
        off = jnp.where(lane < COLS, lane, jnp.where(lane < COLS + 64, -1, COLS))
        col = idx[1] * COLS + off
        for g in range(16):
            m = orders[8 * g : 8 * g + 8, :]
            cos, sin = unit_circle(m * col)
            scale = jnp.where(m > 0, math.sqrt(2.0 / NLON), math.sqrt(1.0 / NLON)).astype(F32)
            hi, lo = split(jnp.concatenate([cos * scale, sin * scale], axis=0))
            harm_ref[16 * g : 16 * g + 16, :] = lo
            harm_ref[272 + 16 * g : 288 + 16 * g, :] = hi
        sub = lax.broadcasted_iota(jnp.int32, (16, COLS + 128), 0)
        lane = lax.broadcasted_iota(jnp.int32, (16, COLS + 128), 1)
        ends = ((sub == 0) & (lane == 0)) | ((sub == 1) & (lane == COLS - 1))
        harm_ref[256:272, :] = jnp.where(ends, 1.0, 0.0).astype(BF16)
        sea = depth_ref[...] * mask
        for r, x in ((16, sea), (17, fric_ref[...])):
            first_ref[r : r + 1, :] = x[:1]
            last_ref[r : r + 1, :] = x[ROWS - 1 :]
        first_ref[18:, :] = jnp.zeros((6, COLS), F32)
        last_ref[18:, :] = jnp.zeros((6, COLS), F32)
        pick = harm_ref[256:272, :COLS]
        hi, lo = split(jnp.concatenate([sea, fric_ref[...]], axis=0))
        edge = lax.dot_general(pick, hi, NT, preferred_element_type=F32)
        edge = edge + lax.dot_general(pick, lo, NT, preferred_element_type=F32)
        cols_ref[:, 1024:] = edge[:8]

    field = jnp.concatenate([elev_ref[c] * mask for c in range(4)], axis=0)
    hi, lo = split(field)
    both = lax.dot_general(harm_ref[:, :COLS], hi, NT, preferred_element_type=F32)
    small = lax.dot_general(harm_ref[256:, :COLS], lo, NT, preferred_element_type=F32)
    out = both[272:] + (both[:256] + small[16:])
    part_ref[...] = (out * PART_SCALE).reshape(16, 16, 256).astype(part_ref.dtype)
    for c in range(4):
        first_ref[pl.ds(4 * i + c, 1), :] = field[64 * c : 64 * c + 1]
        last_ref[pl.ds(4 * i + c, 1), :] = field[64 * c + 63 : 64 * c + 64]
    cols_ref[:, pl.ds(pl.multiple_of(256 * i, 256), 256)] = both[256:264] + small[:8]


def dft(idx, om, elevation, mask, depth, friction, legendre):
    def whole(shape):
        return pl.BlockSpec(shape, lambda i, x: (0,) * len(shape))

    return pl.pallas_call(
        dft_kernel,
        grid_spec=pltpu.PrefetchScalarGridSpec(
            num_scalar_prefetch=1,
            grid=(4,),
            in_specs=[
                whole((1, 128)),
                pl.BlockSpec((4, ROWS, COLS), lambda i, x: (i, 0, 0)),
                whole((ROWS, COLS)),
                whole((ROWS, COLS)),
                whole((ROWS, COLS)),
                pl.BlockSpec((2, ROWS, DEG), lambda i, x: (4 - 4 * x[2] + i, 0, 0)),
            ],
            out_specs=[
                pl.BlockSpec((16, 16, 256), lambda i, x: (0, 0, i)),
                whole((528, COLS + 128)),
                pl.BlockSpec((2, ROWS, DEG), lambda i, x: (i, 0, 0)),
                whole((24, COLS)),
                whole((24, COLS)),
                whole((8, 1152)),
            ],
        ),
        out_shape=[
            jax.ShapeDtypeStruct((16, 16, 1024), F32),
            jax.ShapeDtypeStruct((528, COLS + 128), BF16),
            jax.ShapeDtypeStruct((8, ROWS, DEG), BF16),
            jax.ShapeDtypeStruct((24, COLS), F32),
            jax.ShapeDtypeStruct((24, COLS), F32),
            jax.ShapeDtypeStruct((8, 1152), F32),
        ],
        compiler_params=params(60),
        name="dft",
    )(idx, om, elevation, mask, depth, friction, legendre)


def analyse_kernel(idx, r_ref, own_ref, rcv_ref, *rest):
    outs, (mid_ref, outer_ref, a_ref, e_ref) = rest[-8:-4], rest[-4:]

    @pl.when(pl.program_id(0) == 0)
    def _():
        me = idx[2]
        low = lax.broadcasted_iota(jnp.int32, (16, 128), 1) < 64
        for t in range(8):
            tiles = [r_ref[which, :, 128 * t : 128 * t + 128] for which in (me, 1 - me)]
            f0, f1 = tiles
            even = jnp.where(low, f0, pltpu.roll(f1, 64, 1))
            odd = jnp.where(low, pltpu.roll(f0, 64, 1), f1)
            for ch, val in ((2 * t, even), (2 * t + 1, odd)):
                for p in range(2):
                    a_ref[pl.ds(16 * p + ch, 8, stride=32), :] = val[8 * p : 8 * p + 8, :]

    i = pl.program_id(0)
    pair = (idx[3] + i) & 3
    for s in range(2):
        a = a_ref[pl.ds(pl.multiple_of(64 * pair, 64) + 32 * s, 32), :].astype(BF16)
        table = jnp.concatenate([own_ref[s], rcv_ref[s]], axis=0)
        sums = jnp.dot(a, table, preferred_element_type=F32)
        for k, out_ref in enumerate(outs):

            @pl.when(i == k)
            def _():
                out_ref[s] = sums.astype(out_ref.dtype)

        low = idx[2] == 0
        own_first, own_last = own_ref[s, :16].astype(F32)[:1], own_ref[s, ROWS - 16 :].astype(F32)[15:]
        rcv_first, rcv_last = rcv_ref[s, :16].astype(F32)[:1], rcv_ref[s, ROWS - 16 :].astype(F32)[15:]
        e_ref[pl.ds(2 * pair + s, 1), :] = jnp.where(low, rcv_first, own_first)
        e_ref[pl.ds(8 + 2 * pair + s, 1), :] = jnp.where(low, own_last, rcv_last)
        e_ref[pl.ds(16 + 2 * pair + s, 1), :] = jnp.where(low, own_first, rcv_first)
        e_ref[pl.ds(24 + 2 * pair + s, 1), :] = jnp.where(low, rcv_last, own_last)

    @pl.when(i == 3)
    def _():
        mid_ref[...] = e_ref[:16, :].astype(BF16)
        outer_ref[...] = e_ref[16:, :].astype(BF16)


def analyse(idx, received, legendre, other, after, dtype):
    whole = pl.BlockSpec((2, 32, DEG), lambda i, x: (0, 0, 0))
    return pl.pallas_call(
        analyse_kernel,
        grid_spec=pltpu.PrefetchScalarGridSpec(
            num_scalar_prefetch=1,
            grid=(4,),
            in_specs=[
                pl.BlockSpec((2, 16, 1024), lambda i, x: (0, 0, 0)),
                pl.BlockSpec((2, ROWS, DEG), lambda i, x: (4 * x[2] + ((x[3] + i) & 3), 0, 0)),
                pl.BlockSpec((2, ROWS, DEG), lambda i, x: ((x[3] + i) & 3, 0, 0)),
            ]
            + [pl.BlockSpec(memory_space=pl.ANY)] * len(after),
            out_specs=[
                whole,
                whole,
                whole,
                whole,
                pl.BlockSpec((16, DEG), lambda i, x: (0, 0)),
                pl.BlockSpec((16, DEG), lambda i, x: (0, 0)),
            ],
            scratch_shapes=[pltpu.VMEM((256, 128), F32), pltpu.VMEM((32, DEG), F32)],
        ),
        out_shape=[
            jax.ShapeDtypeStruct((2, 32, DEG), F32),
            jax.ShapeDtypeStruct((2, 32, DEG), dtype),
            jax.ShapeDtypeStruct((2, 32, DEG), dtype),
            jax.ShapeDtypeStruct((2, 32, DEG), dtype),
            jax.ShapeDtypeStruct((16, DEG), BF16),
            jax.ShapeDtypeStruct((16, DEG), BF16),
        ],
        compiler_params=params(),
        name="analyse",
    )(idx, received, legendre, other, *after)


def add_kernel(idx, own_ref, a_ref, b_ref, c_ref, *outs):
    for k, out_ref in enumerate(outs):
        z = (idx[4] + k) & 3
        total = own_ref[z] + a_ref[z].astype(F32) + b_ref[z].astype(F32) + c_ref[z].astype(F32)
        out_ref[...] = total.astype(out_ref.dtype)


def add_bands(idx, own, others, dtype):
    part = pl.BlockSpec((4, 16, DEG), lambda i, x: (0, 0, 0))
    return pl.pallas_call(
        add_kernel,
        grid_spec=pltpu.PrefetchScalarGridSpec(
            num_scalar_prefetch=1,
            grid=(1,),
            in_specs=[part] * 4,
            out_specs=[pl.BlockSpec((16, DEG), lambda i, x: (0, 0))] * 4,
        ),
        out_shape=[jax.ShapeDtypeStruct((16, DEG), t) for t in (F32, dtype, dtype, dtype)],
        compiler_params=params(),
        name="add_bands",
    )(idx, own.reshape(4, 16, DEG), *[x.reshape(4, 16, DEG) for x in others])


def synth_kernel(idx, w0_ref, w1_ref, w2_ref, w3_ref, own_ref, rcv_ref, mid_ref, prev_ref, next_ref, out_ref, sc_ref, t_ref, u_ref):
    edges = jnp.concatenate([mid_ref[...], prev_ref[...], next_ref[...]], axis=0)
    i = pl.program_id(0)
    pair = (idx[3] - i) & 3
    for k, w_ref in enumerate((w0_ref, w1_ref, w2_ref, w3_ref)):

        @pl.when(i == k)
        def _():
            for z in range(4):
                sc_ref[16 * z : 16 * z + 16, :] = w_ref[(idx[4] - z) & 3]

    for s in range(2):
        table = jnp.concatenate([own_ref[s], rcv_ref[s]], axis=0)
        row = pl.multiple_of(64 * pair, 64) + 32 * s
        scaled = sc_ref[32 * s : 32 * s + 32, :]
        t_ref[pl.ds(row, 32), :] = lax.dot_general(scaled, table, NT, preferred_element_type=F32)
        u_ref[2 * pair + s, :, :32] = lax.dot_general(edges, scaled, NT, preferred_element_type=F32)

    @pl.when(i == 3)
    def _():
        me = idx[2]
        lane = lax.broadcasted_iota(jnp.int32, (8, 128), 1)
        sub = lax.broadcasted_iota(jnp.int32, (8, 128), 0)
        low = lane < 64
        for t in range(8):
            own, oth = [], []
            for p in range(2):
                v0 = t_ref[pl.ds(16 * p + 2 * t, 8, stride=32), :]
                v1 = t_ref[pl.ds(16 * p + 2 * t + 1, 8, stride=32), :]
                own.append(jnp.where(low, v0, pltpu.roll(v1, 64, 1)))
                oth.append(jnp.where(low, pltpu.roll(v0, 64, 1), v1))
            own = jnp.concatenate(own, axis=0).astype(out_ref.dtype)
            oth = jnp.concatenate(oth, axis=0).astype(out_ref.dtype)
            for d in range(8):
                out_ref[2 * d + me, :, 128 * t : 128 * t + 128] = own
                out_ref[2 * d + 1 - me, :, 128 * t : 128 * t + 128] = oth
        for half in range(2):
            sides = []
            for side in range(2):
                g = 8 * ((3, 0), (1, 4))[half][side]
                v = jnp.zeros((8, 128), F32)
                for s in range(8):
                    v = jnp.where(sub == s, u_ref[s, g : g + 8, :], v)
                sides.append(v)
            top, bottom = sides
            rows = [
                jnp.where(lane < 16, top, pltpu.roll(bottom, 16, 1)),
                jnp.where(lane < 16, pltpu.roll(top, 112, 1), bottom),
            ]
            rows = [jnp.where(lane < 32, x, 0.0) for x in rows]
            edge = jnp.concatenate(rows, axis=0).astype(out_ref.dtype)
            for d in range(8):
                out_ref[2 * d + half, :, 1024:] = edge


def synthesise(idx, parts, legendre, other, edges, dtype):
    def whole(shape):
        return pl.BlockSpec(shape, lambda i, x: (0,) * len(shape))

    return pl.pallas_call(
        synth_kernel,
        grid_spec=pltpu.PrefetchScalarGridSpec(
            num_scalar_prefetch=1,
            grid=(4,),
            in_specs=[whole((4, 16, DEG))] * 4
            + [
                pl.BlockSpec((2, ROWS, DEG), lambda i, x: (4 * x[2] + ((x[3] - i) & 3), 0, 0)),
                pl.BlockSpec((2, ROWS, DEG), lambda i, x: ((x[3] - i) & 3, 0, 0)),
            ]
            + [whole((16, DEG))] * 3,
            out_specs=whole((16, 16, 1152)),
            scratch_shapes=[
                pltpu.VMEM((64, DEG), BF16),
                pltpu.VMEM((256, 128), F32),
                pltpu.VMEM((8, 48, 128), F32),
            ],
        ),
        out_shape=jax.ShapeDtypeStruct((16, 16, 1152), dtype),
        compiler_params=params(),
        name="synthesise",
    )(idx, *parts, legendre, other, *edges)


def lat_of(row):
    return -LAT_EDGE + row * LAT_STEP


def sweep_kernel(
    idx, g_ref, harm_ref, elev_ref, depth_ref, fric_ref, mask_ref, before_ref, after_ref, west_ref, east_ref, w_ref,
    new_ref, sal_ref, fnew_ref, spad, dpad, fpad, nf, salbuf, lonh_all, sem,
):
    b = pl.program_id(0)
    lat0 = idx[0] * ROWS

    def send(c):
        part = pl.ds(4 * c, 4)
        return pltpu.make_async_copy(salbuf.at[part], sal_ref.at[part], sem.at[c])

    @pl.when(b == 0)
    def _():
        lane = lax.broadcasted_iota(jnp.int32, (8, COLS), 1)
        col = idx[1] * COLS + lane
        c1, s1 = unit_circle(col)
        c2, s2 = unit_circle(2 * col)
        waves = (c2[:1], s2[:1], c1[:1], s1[:1])

        def shapes(first, count):
            row = first.astype(F32) + lax.broadcasted_iota(jnp.int32, (count, 128), 0).astype(F32)
            phi = lat_of(row + 0.5)
            cosphi = jnp.cos(phi)
            return jnp.tile(cosphi * cosphi, (1, 4)), jnp.tile(jnp.sin(2.0 * phi), (1, 4))

        sq, s2phi = shapes(lat0, ROWS)
        up_sq, up_s2 = shapes(lat0 - 1, 8)
        dn_sq, dn_s2 = shapes(lat0 + ROWS, 8)

        def invert(cols):
            part = g_ref[:, cols]
            hi = lax.dot_general(part, harm_ref[272:, :], TN, preferred_element_type=F32)
            lo = lax.dot_general(part, harm_ref[:256, :], TN, preferred_element_type=F32)
            return hi + lo

        sub = lax.broadcasted_iota(jnp.int32, (32, 128), 0) & 15
        lane = lax.broadcasted_iota(jnp.int32, (32, 128), 1)
        place = ((sub == 1) & (lane < 64)) | ((sub == 8) & (lane >= 64))
        place = jnp.where(place, 1.0, 0.0).astype(BF16)
        hi, lo = split(jnp.concatenate([west_ref[...], east_ref[...]], axis=0))
        beside = lax.dot_general(jnp.concatenate([hi, lo], axis=0), place, TN, preferred_element_type=F32)
        for ch in range(18):
            lonh_all[ch] = beside[64 * ch : 64 * ch + 64]
        edge = invert(slice(1024, 1152))
        for ch in range(CH):
            if ch % 4 == 0:
                quarter = invert(slice(64 * ch, 64 * ch + 256))
                for c in range(4):
                    salbuf[ch + c] = quarter[64 * c : 64 * c + 64, :COLS]
                    lonh_all[ch + c] = lonh_all[ch + c] - quarter[64 * c : 64 * c + 64, COLS:]
                send(ch // 4).start()
            k = ch // 2
            wave = waves[(0 if k < 4 else 2) + ch % 2]
            eq = EQ_AMPS[k] * (sq if k < 4 else s2phi) * wave
            spad[ch, 8 : 8 + ROWS, :] = elev_ref[ch] - eq - salbuf[ch]
            up = EQ_AMPS[k] * (up_sq if k < 4 else up_s2)[:1] * wave
            dn = EQ_AMPS[k] * (dn_sq if k < 4 else dn_s2)[:1] * wave
            spad[ch, 7:8, :] = before_ref[ch : ch + 1, :] - up - edge[ch : ch + 1, :COLS]
            spad[ch, 8 + ROWS : 9 + ROWS, :] = after_ref[ch : ch + 1, :] - dn - edge[16 + ch : 17 + ch, :COLS]
        dpad[8 : 8 + ROWS, :] = depth_ref[...] * mask_ref[...].astype(F32)
        fpad[8 : 8 + ROWS, :] = fric_ref[...]
        top = jnp.where(idx[0] == 0, 0.0, 1.0)
        bottom = jnp.where(idx[0] == 31, 0.0, 1.0)
        dpad[7:8, :] = before_ref[16:17, :] * top
        dpad[8 + ROWS : 9 + ROWS, :] = after_ref[16:17, :] * bottom
        fpad[7:8, :] = before_ref[17:18, :]
        fpad[8 + ROWS : 9 + ROWS, :] = after_ref[17:18, :]

        for blk in range(9):
            lo = 8 * blk
            row = (lat0 + lo).astype(F32) + lax.broadcasted_iota(jnp.int32, (8, 128), 0).astype(F32)
            cosf = jnp.tile(jnp.cos(lat_of(row)), (1, 4))
            hh = dpad[8 + lo : 16 + lo, :] * dpad[7 + lo : 15 + lo, :]
            h = jnp.sqrt(hh)
            r = 0.5 * (fpad[8 + lo : 16 + lo, :] + fpad[7 + lo : 15 + lo, :])
            for k in range(8):
                om = FREQUENCIES[k]
                inv = -hh / (r * r + (om * om) * hh)
                rc = inv * r * cosf
                ic = inv * h * om * cosf
                dr = spad[2 * k, 8 + lo : 16 + lo, :] - spad[2 * k, 7 + lo : 15 + lo, :]
                di = spad[2 * k + 1, 8 + lo : 16 + lo, :] - spad[2 * k + 1, 7 + lo : 15 + lo, :]
                nf[2 * k, lo : lo + 8, :] = rc * dr - ic * di
                nf[2 * k + 1, lo : lo + 8, :] = rc * di + ic * dr

    base = pl.multiple_of(8 * b, 8)
    own = pl.ds(base + 8, 8)
    row = (lat0 + base).astype(F32) + lax.broadcasted_iota(jnp.int32, (8, 128), 0).astype(F32)
    phi = lat_of(row + 0.5)
    rcos1 = 1.0 / jnp.cos(phi)
    rcos = jnp.tile(rcos1, (1, 4))
    lane = lax.broadcasted_iota(jnp.int32, (8, COLS), 1)
    last = lane == COLS - 1
    first = lane == 0
    tile_lane = lax.broadcasted_iota(jnp.int32, (8, 128), 1)
    col = idx[1] * COLS + jnp.where(tile_lane < 64, -1, COLS)
    c1, s1 = unit_circle(col)
    c2, s2 = unit_circle(2 * col)
    waves = (c2, s2, c1, s1)
    cosphi = jnp.cos(phi)
    sq, s2phi = cosphi * cosphi, jnp.sin(2.0 * phi)

    def east_of(x, halo):
        wide = jnp.tile(halo, (1, 4))
        return jnp.where(last, wide, pltpu.roll(x, COLS - 1, 1))

    d = dpad[own, :]
    f = fpad[own, :]
    dh = lonh_all[16, pl.ds(base, 8), :]
    fh = lonh_all[17, pl.ds(base, 8), :]
    hh = d * east_of(d, dh)
    h = jnp.sqrt(hh)
    r = 0.5 * (f + east_of(f, fh))
    hhw = d[:, :128] * dh
    hw = jnp.sqrt(hhw)
    rw = 0.5 * (f[:, :128] + fh)
    mask = mask_ref[pl.ds(base, 8), :].astype(F32)
    ecell, ncell = [], []
    for k in range(8):
        om = FREQUENCIES[k]
        inv = -hh / (r * r + (om * om) * hh)
        rc = inv * r * rcos
        ic = inv * h * om * rcos
        invw = -hhw / (rw * rw + (om * om) * hhw)
        rcw = invw * rw * rcos1
        icw = invw * hw * om * rcos1
        diffs, wdiffs = [], []
        for ch in (2 * k, 2 * k + 1):
            s = spad[ch, own, :]
            eq = EQ_AMPS[k] * (sq if k < 4 else s2phi) * waves[(0 if k < 4 else 2) + ch % 2]
            sh = lonh_all[ch, pl.ds(base, 8), :] - eq
            diffs.append(east_of(s, sh) - s)
            wdiffs.append(s[:, :128] - sh)
        flux = (rc * diffs[0] - ic * diffs[1], rc * diffs[1] + ic * diffs[0])
        fluxw = (rcw * wdiffs[0] - icw * wdiffs[1], rcw * wdiffs[1] + icw * wdiffs[0])
        div = []
        for p in range(2):
            ch = 2 * k + p
            west = jnp.where(first, jnp.tile(fluxw[p], (1, 4)), pltpu.roll(flux[p], 1, 1))
            south = nf[ch, pl.ds(base, 8), :]
            below = nf[ch, pl.ds(base + 8, 8), :]
            sub = lax.broadcasted_iota(jnp.int32, (8, COLS), 0)
            north = pltpu.roll(jnp.where(sub == 0, below, south), 7, 0)
            div.append((flux[p] - west + (north - south)) * rcos)
            ecell.append(0.5 * (flux[p] + west))
            ncell.append(0.5 * (north + south))
        cr = elev_ref[2 * k, pl.ds(base, 8), :]
        ci = elev_ref[2 * k + 1, pl.ds(base, 8), :]
        new_ref[2 * k] = (cr - RELAX_RATE * (div[0] + om * ci)) * mask
        new_ref[2 * k + 1] = (ci - RELAX_RATE * (div[1] - om * cr)) * mask

    def stacked(parts):
        hi, lo = split(jnp.concatenate(parts, axis=0))
        return jnp.concatenate([hi, lo], axis=0)

    xe, xn = stacked(ecell), stacked(ncell)
    total = jnp.zeros((8, COLS), F32)
    for q in range(4):
        w = w_ref[128 * q : 128 * q + 128, :]
        u = jnp.dot(w, xe, preferred_element_type=F32)
        v = jnp.dot(w, xn, preferred_element_type=F32)
        x = u * u + v * v + SPEED_EPS * SPEED_EPS
        speed = x * lax.rsqrt(x)
        for s in range(16):
            total = total + speed[8 * s : 8 * s + 8, :]
    fnew_ref[...] = BASE_FRICTION + DRAG_COEFF * total / SAMPLES

    @pl.when(b == 7)
    def _():
        for c in range(4):
            send(c).wait()


def sample_matrix():
    time = (STEP_TIME * np.arange(SAMPLES, dtype=np.float32))[:, None]
    phases = time * np.asarray(FREQUENCIES, np.float32)[None, :]
    table = np.stack([np.cos(phases), np.sin(phases)], axis=2).reshape(SAMPLES, CH).astype(np.float32)
    hi = table.astype(jnp.bfloat16)
    eye = np.eye(8, dtype=np.float32)
    wide = [np.kron(x.astype(np.float32), eye) for x in (hi, hi)]
    return jnp.asarray(np.concatenate(wide, axis=1), BF16)


def sweep(idx, g, harm, elevation, depth, friction, mask, before, after, west, east, w):
    def whole(shape):
        return pl.BlockSpec(shape, lambda i, x: (0,) * len(shape))

    return pl.pallas_call(
        sweep_kernel,
        grid_spec=pltpu.PrefetchScalarGridSpec(
            num_scalar_prefetch=1,
            grid=(8,),
            in_specs=[
                whole((256, 1152)),
                whole((528, COLS + 128)),
                whole((CH, ROWS, COLS)),
                whole((ROWS, COLS)),
                whole((ROWS, COLS)),
                whole((ROWS, COLS)),
                whole((24, COLS)),
                whole((24, COLS)),
                whole((8, 1152)),
                whole((8, 1152)),
                whole((512, 256)),
            ],
            out_specs=[
                pl.BlockSpec((CH, 8, COLS), lambda i, x: (0, i, 0)),
                pl.BlockSpec(memory_space=pl.ANY),
                pl.BlockSpec((8, COLS), lambda i, x: (i, 0)),
            ],
            scratch_shapes=[
                pltpu.VMEM((CH, 80, COLS), F32),
                pltpu.VMEM((80, COLS), F32),
                pltpu.VMEM((80, COLS), F32),
                pltpu.VMEM((CH, 72, COLS), F32),
                pltpu.VMEM((CH, ROWS, COLS), F32),
                pltpu.VMEM((CH + 2, ROWS, 128), F32),
                pltpu.SemaphoreType.DMA((4,)),
            ],
        ),
        out_shape=[
            jax.ShapeDtypeStruct((CH, ROWS, COLS), F32),
            jax.ShapeDtypeStruct((CH, ROWS, COLS), F32),
            jax.ShapeDtypeStruct((ROWS, COLS), F32),
        ],
        compiler_params=params(),
        name="sweep",
    )(idx, g, harm, elevation, depth, friction, mask, before, after, west, east, w)


LAT = ("zh", "x", "c")
LON = ("y", "zl")


def shift(value, axes, size, step):
    return lax.ppermute(value, axes, [(i, (i + step) % size) for i in range(size)])


def shift_lat(value, step):
    return lax.ppermute(value, LAT, [(i, i + step) for i in range(32) if 0 <= i + step < 32])


def all_shifts(values, axis):
    return [shift(value, axis, 4, k + 1) for k, value in enumerate(values)]


def swap(x, axis):
    return lax.all_to_all(x, axis, 0, 0, tiled=True)


def on_device(elevation, depth, friction, land_mask, order_map, legendre, load):
    lat = lax.axis_index(LAT)
    lon = lax.axis_index(LON)
    core = lax.axis_index("c")
    x, z = lax.axis_index("x"), lax.axis_index("zh")
    idx = jnp.stack([lat, lon, core, x, z]).astype(jnp.int32)

    part, harm, half, first_row, last_row, ends = dft(
        idx, order_map[None, :], elevation, land_mask, depth, friction, legendre
    )
    received = swap(part.astype(jnp.float16), ("y", "zl", "c"))
    other = shift(half, "c", 2, 1)
    before = shift_lat(last_row, 1)
    after = shift_lat(first_row, -1)
    west = shift(ends, LON, 8, 1)
    east = shift(ends, LON, 8, -1)
    fourier = jnp.sum(received.reshape(8, 2, 16, 1024).astype(F32), axis=0) * (1.0 / PART_SCALE)
    own, *parts, mid, outer = analyse(idx, fourier, legendre, other, (before, after, west, east), BF16)
    prior = shift_lat(outer, 2)
    later = shift_lat(outer, -2)

    own, *parts = add_bands(idx, own, all_shifts(parts, "x"), BF16)
    total = own + sum(part.astype(F32) for part in all_shifts(parts, "zh"))
    scaled = (total * load[None, :]).astype(BF16)
    by_z = jnp.stack([scaled, *all_shifts([scaled] * 3, "zh")])
    spread = synthesise(
        idx, [by_z, *all_shifts([by_z] * 3, "x")], legendre, other, (mid, prior, later), BF16
    )
    g = swap(spread, ("y", "zl", "c"))
    new, sal, fnew = sweep(
        idx, g.reshape(256, 1152), harm, elevation, depth, friction, land_mask,
        before, after, west, east, sample_matrix(),
    )
    return new, sal, fnew


def solution(mesh):
    fine = Mesh(mesh.devices.reshape(4, 4, 2, 4, 2), ("zh", "x", "c", "y", "zl"))
    return jax.shard_map(
        on_device,
        mesh=fine,
        in_specs=(
            P(None, LAT, LON),
            P(LAT, LON),
            P(LAT, LON),
            P(LAT, LON),
            P(),
            P(LON, LAT, None),
            P(),
        ),
        out_specs=(P(None, LAT, LON), P(None, LAT, LON), P(LAT, LON)),
        check_vma=False,
    )
```

```python
import functools
import math

import jax
import jax.numpy as jnp
import numpy as np
from jax import lax
from jax.experimental import pallas as pl
from jax.experimental.pallas import tpu as pltpu
from jax.sharding import Mesh, PartitionSpec as P

SAMPLES = 64
FREQUENCIES = (1.0, 1.0347, 0.9582, 1.0379, 0.5018, 0.4651, 0.4986, 0.4482)
EQ_AMPS = (0.73, 0.34, 0.14, 0.09, 0.42, 0.3, 0.14, 0.06)
LAT_EDGE = 1.3614
RELAX_RATE = 0.1
BASE_FRICTION = 0.05
DRAG_COEFF = 0.5
SPEED_EPS = 0.001
STEP_TIME = 3.0
NLAT = 2048
NLON = 4096
LAT_STEP = 2.0 * LAT_EDGE / NLAT
ROWS = 64
COLS = 512
CH = 16
DEG = 2048
F32 = jnp.float32
BF16 = jnp.bfloat16
PART_SCALE = 512.0


def params(mib=24):
    return pltpu.CompilerParams(vmem_limit_bytes=mib * 1024 * 1024)


def unit_circle(k):
    k = k & (NLON - 1)
    quad = (k + 512) >> 10
    t = (k - (quad << 10)).astype(F32) * (2.0 * math.pi / NLON)
    q = quad & 3
    t2 = t * t
    s = t * (1.0 + t2 * (-1.0 / 6 + t2 * (1.0 / 120 + t2 * (-1.0 / 5040 + t2 * (1.0 / 362880)))))
    c = 1.0 + t2 * (-0.5 + t2 * (1.0 / 24 + t2 * (-1.0 / 720 + t2 * (1.0 / 40320))))
    swap = (q & 1) == 1
    cos = jnp.where(swap, s, c)
    sin = jnp.where(swap, c, s)
    cos = jnp.where((q == 1) | (q == 2), -cos, cos)
    sin = jnp.where(q >= 2, -sin, sin)
    return cos, sin


def split(x):
    hi = x.astype(BF16)
    lo = (x - hi.astype(F32)).astype(BF16)
    return hi, lo


NT = (((1,), (1,)), ((), ()))
TN = (((0,), (0,)), ((), ()))


def dft_kernel(
    idx, om_ref, elev_ref, mask_ref, depth_ref, fric_ref, leg_ref,
    part_ref, harm_ref, half_ref, first_ref, last_ref, cols_ref,
):
    i = pl.program_id(0)
    half_ref[...] = leg_ref[...]
    mask = mask_ref[...].astype(F32)
    @pl.when(i == 0)
    def _():
        diag = lax.broadcasted_iota(jnp.int32, (128, 128), 0) == lax.broadcasted_iota(jnp.int32, (128, 128), 1)
        orders = jnp.broadcast_to(om_ref[...].astype(F32), (128, 128))
        orders = jnp.sum(jnp.where(diag, orders, 0.0), axis=1, keepdims=True).astype(jnp.int32)
        lane = lax.broadcasted_iota(jnp.int32, (8, COLS + 128), 1)
        off = jnp.where(lane < COLS, lane, jnp.where(lane < COLS + 64, -1, COLS))
        col = idx[1] * COLS + off
        for g in range(16):
            m = orders[8 * g : 8 * g + 8, :]
            cos, sin = unit_circle(m * col)
            scale = jnp.where(m > 0, math.sqrt(2.0 / NLON), math.sqrt(1.0 / NLON)).astype(F32)
            hi, lo = split(jnp.concatenate([cos * scale, sin * scale], axis=0))
            harm_ref[16 * g : 16 * g + 16, :] = lo
            harm_ref[272 + 16 * g : 288 + 16 * g, :] = hi
        sub = lax.broadcasted_iota(jnp.int32, (16, COLS + 128), 0)
        lane = lax.broadcasted_iota(jnp.int32, (16, COLS + 128), 1)
        ends = ((sub == 0) & (lane == 0)) | ((sub == 1) & (lane == COLS - 1))
        harm_ref[256:272, :] = jnp.where(ends, 1.0, 0.0).astype(BF16)
        sea = depth_ref[...] * mask
        for r, x in ((16, sea), (17, fric_ref[...])):
            first_ref[r : r + 1, :] = x[:1]
            last_ref[r : r + 1, :] = x[ROWS - 1 :]
        first_ref[18:, :] = jnp.zeros((6, COLS), F32)
        last_ref[18:, :] = jnp.zeros((6, COLS), F32)
        pick = harm_ref[256:272, :COLS]
        hi, lo = split(jnp.concatenate([sea, fric_ref[...]], axis=0))
        edge = lax.dot_general(pick, hi, NT, preferred_element_type=F32)
        edge = edge + lax.dot_general(pick, lo, NT, preferred_element_type=F32)
        cols_ref[:, 1024:] = edge[:8]

    field = jnp.concatenate([elev_ref[c] * mask for c in range(4)], axis=0)
    hi, lo = split(field)
    both = lax.dot_general(harm_ref[:, :COLS], hi, NT, preferred_element_type=F32)
    small = lax.dot_general(harm_ref[256:, :COLS], lo, NT, preferred_element_type=F32)
    out = both[272:] + (both[:256] + small[16:])
    part_ref[...] = (out * PART_SCALE).reshape(16, 16, 256).astype(part_ref.dtype)
    for c in range(4):
        first_ref[pl.ds(4 * i + c, 1), :] = field[64 * c : 64 * c + 1]
        last_ref[pl.ds(4 * i + c, 1), :] = field[64 * c + 63 : 64 * c + 64]
    cols_ref[:, pl.ds(pl.multiple_of(256 * i, 256), 256)] = both[256:264] + small[:8]


def dft(idx, om, elevation, mask, depth, friction, legendre):
    def whole(shape):
        return pl.BlockSpec(shape, lambda i, x: (0,) * len(shape))

    return pl.pallas_call(
        dft_kernel,
        grid_spec=pltpu.PrefetchScalarGridSpec(
            num_scalar_prefetch=1,
            grid=(4,),
            in_specs=[
                whole((1, 128)),
                pl.BlockSpec((4, ROWS, COLS), lambda i, x: (i, 0, 0)),
                whole((ROWS, COLS)),
                whole((ROWS, COLS)),
                whole((ROWS, COLS)),
                pl.BlockSpec((2, ROWS, DEG), lambda i, x: (4 - 4 * x[2] + i, 0, 0)),
            ],
            out_specs=[
                pl.BlockSpec((16, 16, 256), lambda i, x: (0, 0, i)),
                whole((528, COLS + 128)),
                pl.BlockSpec((2, ROWS, DEG), lambda i, x: (i, 0, 0)),
                whole((24, COLS)),
                whole((24, COLS)),
                whole((8, 1152)),
            ],
        ),
        out_shape=[
            jax.ShapeDtypeStruct((16, 16, 1024), F32),
            jax.ShapeDtypeStruct((528, COLS + 128), BF16),
            jax.ShapeDtypeStruct((8, ROWS, DEG), BF16),
            jax.ShapeDtypeStruct((24, COLS), F32),
            jax.ShapeDtypeStruct((24, COLS), F32),
            jax.ShapeDtypeStruct((8, 1152), F32),
        ],
        compiler_params=params(60),
        name="dft",
    )(idx, om, elevation, mask, depth, friction, legendre)


def analyse_kernel(idx, r_ref, own_ref, rcv_ref, *rest):
    outs, (mid_ref, outer_ref, a_ref, e_ref) = rest[-8:-4], rest[-4:]

    @pl.when(pl.program_id(0) == 0)
    def _():
        me = idx[2]
        low = lax.broadcasted_iota(jnp.int32, (16, 128), 1) < 64
        for t in range(8):
            tiles = [r_ref[which, :, 128 * t : 128 * t + 128] for which in (me, 1 - me)]
            f0, f1 = tiles
            even = jnp.where(low, f0, pltpu.roll(f1, 64, 1))
            odd = jnp.where(low, pltpu.roll(f0, 64, 1), f1)
            for ch, val in ((2 * t, even), (2 * t + 1, odd)):
                for p in range(2):
                    a_ref[pl.ds(16 * p + ch, 8, stride=32), :] = val[8 * p : 8 * p + 8, :]

    i = pl.program_id(0)
    pair = (idx[3] + i) & 3
    for s in range(2):
        a = a_ref[pl.ds(pl.multiple_of(64 * pair, 64) + 32 * s, 32), :].astype(BF16)
        table = jnp.concatenate([own_ref[s], rcv_ref[s]], axis=0)
        sums = jnp.dot(a, table, preferred_element_type=F32)
        for k, out_ref in enumerate(outs):

            @pl.when(i == k)
            def _():
                out_ref[s] = sums.astype(out_ref.dtype)

        low = idx[2] == 0
        own_first, own_last = own_ref[s, :16].astype(F32)[:1], own_ref[s, ROWS - 16 :].astype(F32)[15:]
        rcv_first, rcv_last = rcv_ref[s, :16].astype(F32)[:1], rcv_ref[s, ROWS - 16 :].astype(F32)[15:]
        e_ref[pl.ds(2 * pair + s, 1), :] = jnp.where(low, rcv_first, own_first)
        e_ref[pl.ds(8 + 2 * pair + s, 1), :] = jnp.where(low, own_last, rcv_last)
        e_ref[pl.ds(16 + 2 * pair + s, 1), :] = jnp.where(low, own_first, rcv_first)
        e_ref[pl.ds(24 + 2 * pair + s, 1), :] = jnp.where(low, rcv_last, own_last)

    @pl.when(i == 3)
    def _():
        mid_ref[...] = e_ref[:16, :].astype(BF16)
        outer_ref[...] = e_ref[16:, :].astype(BF16)


def analyse(idx, received, legendre, other, after, dtype):
    whole = pl.BlockSpec((2, 32, DEG), lambda i, x: (0, 0, 0))
    return pl.pallas_call(
        analyse_kernel,
        grid_spec=pltpu.PrefetchScalarGridSpec(
            num_scalar_prefetch=1,
            grid=(4,),
            in_specs=[
                pl.BlockSpec((2, 16, 1024), lambda i, x: (0, 0, 0)),
                pl.BlockSpec((2, ROWS, DEG), lambda i, x: (4 * x[2] + ((x[3] + i) & 3), 0, 0)),
                pl.BlockSpec((2, ROWS, DEG), lambda i, x: ((x[3] + i) & 3, 0, 0)),
            ]
            + [pl.BlockSpec(memory_space=pl.ANY)] * len(after),
            out_specs=[
                whole,
                whole,
                whole,
                whole,
                pl.BlockSpec((16, DEG), lambda i, x: (0, 0)),
                pl.BlockSpec((16, DEG), lambda i, x: (0, 0)),
            ],
            scratch_shapes=[pltpu.VMEM((256, 128), F32), pltpu.VMEM((32, DEG), F32)],
        ),
        out_shape=[
            jax.ShapeDtypeStruct((2, 32, DEG), F32),
            jax.ShapeDtypeStruct((2, 32, DEG), dtype),
            jax.ShapeDtypeStruct((2, 32, DEG), dtype),
            jax.ShapeDtypeStruct((2, 32, DEG), dtype),
            jax.ShapeDtypeStruct((16, DEG), BF16),
            jax.ShapeDtypeStruct((16, DEG), BF16),
        ],
        compiler_params=params(),
        name="analyse",
    )(idx, received, legendre, other, *after)


def add_kernel(idx, own_ref, a_ref, b_ref, c_ref, *outs):
    for k, out_ref in enumerate(outs):
        z = (idx[4] + k) & 3
        total = own_ref[z] + a_ref[z].astype(F32) + b_ref[z].astype(F32) + c_ref[z].astype(F32)
        out_ref[...] = total.astype(out_ref.dtype)


def add_bands(idx, own, others, dtype):
    part = pl.BlockSpec((4, 16, DEG), lambda i, x: (0, 0, 0))
    return pl.pallas_call(
        add_kernel,
        grid_spec=pltpu.PrefetchScalarGridSpec(
            num_scalar_prefetch=1,
            grid=(1,),
            in_specs=[part] * 4,
            out_specs=[pl.BlockSpec((16, DEG), lambda i, x: (0, 0))] * 4,
        ),
        out_shape=[jax.ShapeDtypeStruct((16, DEG), t) for t in (F32, dtype, dtype, dtype)],
        compiler_params=params(),
        name="add_bands",
    )(idx, own.reshape(4, 16, DEG), *[x.reshape(4, 16, DEG) for x in others])


def synth_kernel(idx, w0_ref, w1_ref, w2_ref, w3_ref, own_ref, rcv_ref, mid_ref, prev_ref, next_ref, out_ref, sc_ref, t_ref, u_ref):
    edges = jnp.concatenate([mid_ref[...], prev_ref[...], next_ref[...]], axis=0)
    i = pl.program_id(0)
    pair = (idx[3] - i) & 3
    for k, w_ref in enumerate((w0_ref, w1_ref, w2_ref, w3_ref)):

        @pl.when(i == k)
        def _():
            for z in range(4):
                sc_ref[16 * z : 16 * z + 16, :] = w_ref[(idx[4] - z) & 3]

    for s in range(2):
        table = jnp.concatenate([own_ref[s], rcv_ref[s]], axis=0)
        row = pl.multiple_of(64 * pair, 64) + 32 * s
        scaled = sc_ref[32 * s : 32 * s + 32, :]
        t_ref[pl.ds(row, 32), :] = lax.dot_general(scaled, table, NT, preferred_element_type=F32)
        u_ref[2 * pair + s, :, :32] = lax.dot_general(edges, scaled, NT, preferred_element_type=F32)

    @pl.when(i == 3)
    def _():
        me = idx[2]
        lane = lax.broadcasted_iota(jnp.int32, (8, 128), 1)
        sub = lax.broadcasted_iota(jnp.int32, (8, 128), 0)
        low = lane < 64
        for t in range(8):
            own, oth = [], []
            for p in range(2):
                v0 = t_ref[pl.ds(16 * p + 2 * t, 8, stride=32), :]
                v1 = t_ref[pl.ds(16 * p + 2 * t + 1, 8, stride=32), :]
                own.append(jnp.where(low, v0, pltpu.roll(v1, 64, 1)))
                oth.append(jnp.where(low, pltpu.roll(v0, 64, 1), v1))
            own = jnp.concatenate(own, axis=0).astype(out_ref.dtype)
            oth = jnp.concatenate(oth, axis=0).astype(out_ref.dtype)
            for d in range(8):
                out_ref[2 * d + me, :, 128 * t : 128 * t + 128] = own
                out_ref[2 * d + 1 - me, :, 128 * t : 128 * t + 128] = oth
        for half in range(2):
            sides = []
            for side in range(2):
                g = 8 * ((3, 0), (1, 4))[half][side]
                v = jnp.zeros((8, 128), F32)
                for s in range(8):
                    v = jnp.where(sub == s, u_ref[s, g : g + 8, :], v)
                sides.append(v)
            top, bottom = sides
            rows = [
                jnp.where(lane < 16, top, pltpu.roll(bottom, 16, 1)),
                jnp.where(lane < 16, pltpu.roll(top, 112, 1), bottom),
            ]
            rows = [jnp.where(lane < 32, x, 0.0) for x in rows]
            edge = jnp.concatenate(rows, axis=0).astype(out_ref.dtype)
            for d in range(8):
                out_ref[2 * d + half, :, 1024:] = edge


def synthesise(idx, parts, legendre, other, edges, dtype):
    def whole(shape):
        return pl.BlockSpec(shape, lambda i, x: (0,) * len(shape))

    return pl.pallas_call(
        synth_kernel,
        grid_spec=pltpu.PrefetchScalarGridSpec(
            num_scalar_prefetch=1,
            grid=(4,),
            in_specs=[whole((4, 16, DEG))] * 4
            + [
                pl.BlockSpec((2, ROWS, DEG), lambda i, x: (4 * x[2] + ((x[3] - i) & 3), 0, 0)),
                pl.BlockSpec((2, ROWS, DEG), lambda i, x: ((x[3] - i) & 3, 0, 0)),
            ]
            + [whole((16, DEG))] * 3,
            out_specs=whole((16, 16, 1152)),
            scratch_shapes=[
                pltpu.VMEM((64, DEG), BF16),
                pltpu.VMEM((256, 128), F32),
                pltpu.VMEM((8, 48, 128), F32),
            ],
        ),
        out_shape=jax.ShapeDtypeStruct((16, 16, 1152), dtype),
        compiler_params=params(),
        name="synthesise",
    )(idx, *parts, legendre, other, *edges)


def lat_of(row):
    return -LAT_EDGE + row * LAT_STEP


def sweep_kernel(
    idx, g_ref, harm_ref, elev_ref, depth_ref, fric_ref, mask_ref, before_ref, after_ref, west_ref, east_ref, w_ref,
    new_ref, sal_ref, fnew_ref, spad, dpad, fpad, nf, salbuf, lonh_all, sem,
):
    b = pl.program_id(0)
    lat0 = idx[0] * ROWS

    def send(c):
        part = pl.ds(4 * c, 4)
        return pltpu.make_async_copy(salbuf.at[part], sal_ref.at[part], sem.at[c])

    @pl.when(b == 0)
    def _():
        lane = lax.broadcasted_iota(jnp.int32, (8, COLS), 1)
        col = idx[1] * COLS + lane
        c1, s1 = unit_circle(col)
        c2, s2 = unit_circle(2 * col)
        waves = (c2[:1], s2[:1], c1[:1], s1[:1])

        def shapes(first, count):
            row = first.astype(F32) + lax.broadcasted_iota(jnp.int32, (count, 128), 0).astype(F32)
            phi = lat_of(row + 0.5)
            cosphi = jnp.cos(phi)
            return jnp.tile(cosphi * cosphi, (1, 4)), jnp.tile(jnp.sin(2.0 * phi), (1, 4))

        sq, s2phi = shapes(lat0, ROWS)
        up_sq, up_s2 = shapes(lat0 - 1, 8)
        dn_sq, dn_s2 = shapes(lat0 + ROWS, 8)

        def invert(cols):
            part = g_ref[:, cols]
            hi = lax.dot_general(part, harm_ref[272:, :], TN, preferred_element_type=F32)
            lo = lax.dot_general(part, harm_ref[:256, :], TN, preferred_element_type=F32)
            return hi + lo

        sub = lax.broadcasted_iota(jnp.int32, (32, 128), 0) & 15
        lane = lax.broadcasted_iota(jnp.int32, (32, 128), 1)
        place = ((sub == 1) & (lane < 64)) | ((sub == 8) & (lane >= 64))
        place = jnp.where(place, 1.0, 0.0).astype(BF16)
        hi, lo = split(jnp.concatenate([west_ref[...], east_ref[...]], axis=0))
        beside = lax.dot_general(jnp.concatenate([hi, lo], axis=0), place, TN, preferred_element_type=F32)
        for ch in range(18):
            lonh_all[ch] = beside[64 * ch : 64 * ch + 64]
        edge = invert(slice(1024, 1152))
        for ch in range(CH):
            if ch % 4 == 0:
                quarter = invert(slice(64 * ch, 64 * ch + 256))
                for c in range(4):
                    salbuf[ch + c] = quarter[64 * c : 64 * c + 64, :COLS]
                    lonh_all[ch + c] = lonh_all[ch + c] - quarter[64 * c : 64 * c + 64, COLS:]
                send(ch // 4).start()
            k = ch // 2
            wave = waves[(0 if k < 4 else 2) + ch % 2]
            eq = EQ_AMPS[k] * (sq if k < 4 else s2phi) * wave
            spad[ch, 8 : 8 + ROWS, :] = elev_ref[ch] - eq - salbuf[ch]
            up = EQ_AMPS[k] * (up_sq if k < 4 else up_s2)[:1] * wave
            dn = EQ_AMPS[k] * (dn_sq if k < 4 else dn_s2)[:1] * wave
            spad[ch, 7:8, :] = before_ref[ch : ch + 1, :] - up - edge[ch : ch + 1, :COLS]
            spad[ch, 8 + ROWS : 9 + ROWS, :] = after_ref[ch : ch + 1, :] - dn - edge[16 + ch : 17 + ch, :COLS]
        dpad[8 : 8 + ROWS, :] = depth_ref[...] * mask_ref[...].astype(F32)
        fpad[8 : 8 + ROWS, :] = fric_ref[...]
        top = jnp.where(idx[0] == 0, 0.0, 1.0)
        bottom = jnp.where(idx[0] == 31, 0.0, 1.0)
        dpad[7:8, :] = before_ref[16:17, :] * top
        dpad[8 + ROWS : 9 + ROWS, :] = after_ref[16:17, :] * bottom
        fpad[7:8, :] = before_ref[17:18, :]
        fpad[8 + ROWS : 9 + ROWS, :] = after_ref[17:18, :]

        for blk in range(9):
            lo = 8 * blk
            row = (lat0 + lo).astype(F32) + lax.broadcasted_iota(jnp.int32, (8, 128), 0).astype(F32)
            cosf = jnp.tile(jnp.cos(lat_of(row)), (1, 4))
            hh = dpad[8 + lo : 16 + lo, :] * dpad[7 + lo : 15 + lo, :]
            h = jnp.sqrt(hh)
            r = 0.5 * (fpad[8 + lo : 16 + lo, :] + fpad[7 + lo : 15 + lo, :])
            for k in range(8):
                om = FREQUENCIES[k]
                inv = -hh / (r * r + (om * om) * hh)
                rc = inv * r * cosf
                ic = inv * h * om * cosf
                dr = spad[2 * k, 8 + lo : 16 + lo, :] - spad[2 * k, 7 + lo : 15 + lo, :]
                di = spad[2 * k + 1, 8 + lo : 16 + lo, :] - spad[2 * k + 1, 7 + lo : 15 + lo, :]
                nf[2 * k, lo : lo + 8, :] = rc * dr - ic * di
                nf[2 * k + 1, lo : lo + 8, :] = rc * di + ic * dr

    def sweep_rows(sub_block):
        out = slice(8 * sub_block, 8 * sub_block + 8)
        base = pl.multiple_of(8 * (2 * b + sub_block), 8)
        own = pl.ds(base + 8, 8)
        row = (lat0 + base).astype(F32) + lax.broadcasted_iota(jnp.int32, (8, 128), 0).astype(F32)
        phi = lat_of(row + 0.5)
        rcos1 = 1.0 / jnp.cos(phi)
        rcos = jnp.tile(rcos1, (1, 4))
        lane = lax.broadcasted_iota(jnp.int32, (8, COLS), 1)
        last = lane == COLS - 1
        first = lane == 0
        tile_lane = lax.broadcasted_iota(jnp.int32, (8, 128), 1)
        col = idx[1] * COLS + jnp.where(tile_lane < 64, -1, COLS)
        c1, s1 = unit_circle(col)
        c2, s2 = unit_circle(2 * col)
        waves = (c2, s2, c1, s1)
        cosphi = jnp.cos(phi)
        sq, s2phi = cosphi * cosphi, jnp.sin(2.0 * phi)

        def east_of(x, halo):
            wide = jnp.tile(halo, (1, 4))
            return jnp.where(last, wide, pltpu.roll(x, COLS - 1, 1))

        d = dpad[own, :]
        f = fpad[own, :]
        dh = lonh_all[16, pl.ds(base, 8), :]
        fh = lonh_all[17, pl.ds(base, 8), :]
        hh = d * east_of(d, dh)
        h = jnp.sqrt(hh)
        r = 0.5 * (f + east_of(f, fh))
        hhw = d[:, :128] * dh
        hw = jnp.sqrt(hhw)
        rw = 0.5 * (f[:, :128] + fh)
        mask = mask_ref[pl.ds(base, 8), :].astype(F32)
        ecell, ncell = [], []
        for k in range(8):
            om = FREQUENCIES[k]
            inv = -hh / (r * r + (om * om) * hh)
            rc = inv * r * rcos
            ic = inv * h * om * rcos
            invw = -hhw / (rw * rw + (om * om) * hhw)
            rcw = invw * rw * rcos1
            icw = invw * hw * om * rcos1
            diffs, wdiffs = [], []
            for ch in (2 * k, 2 * k + 1):
                s = spad[ch, own, :]
                eq = EQ_AMPS[k] * (sq if k < 4 else s2phi) * waves[(0 if k < 4 else 2) + ch % 2]
                sh = lonh_all[ch, pl.ds(base, 8), :] - eq
                diffs.append(east_of(s, sh) - s)
                wdiffs.append(s[:, :128] - sh)
            flux = (rc * diffs[0] - ic * diffs[1], rc * diffs[1] + ic * diffs[0])
            fluxw = (rcw * wdiffs[0] - icw * wdiffs[1], rcw * wdiffs[1] + icw * wdiffs[0])
            div = []
            for p in range(2):
                ch = 2 * k + p
                west = jnp.where(first, jnp.tile(fluxw[p], (1, 4)), pltpu.roll(flux[p], 1, 1))
                south = nf[ch, pl.ds(base, 8), :]
                below = nf[ch, pl.ds(base + 8, 8), :]
                sub = lax.broadcasted_iota(jnp.int32, (8, COLS), 0)
                north = pltpu.roll(jnp.where(sub == 0, below, south), 7, 0)
                div.append((flux[p] - west + (north - south)) * rcos)
                ecell.append(0.5 * (flux[p] + west))
                ncell.append(0.5 * (north + south))
            cr = elev_ref[2 * k, pl.ds(base, 8), :]
            ci = elev_ref[2 * k + 1, pl.ds(base, 8), :]
            new_ref[2 * k, out] = (cr - RELAX_RATE * (div[0] + om * ci)) * mask
            new_ref[2 * k + 1, out] = (ci - RELAX_RATE * (div[1] - om * cr)) * mask

        def stacked(parts):
            hi, lo = split(jnp.concatenate(parts, axis=0))
            return jnp.concatenate([hi, lo], axis=0)

        xe, xn = stacked(ecell), stacked(ncell)
        total = jnp.zeros((8, COLS), F32)
        for q in range(4):
            w = w_ref[128 * q : 128 * q + 128, :]
            u = jnp.dot(w, xe, preferred_element_type=F32)
            v = jnp.dot(w, xn, preferred_element_type=F32)
            x = u * u + v * v + SPEED_EPS * SPEED_EPS
            speed = x * lax.rsqrt(x)
            for s in range(16):
                total = total + speed[8 * s : 8 * s + 8, :]
        fnew_ref[out, :] = BASE_FRICTION + DRAG_COEFF * total / SAMPLES

    for sub_block in range(2):
        sweep_rows(sub_block)

    @pl.when(b == 3)
    def _():
        for c in range(4):
            send(c).wait()


def sample_matrix():
    time = (STEP_TIME * np.arange(SAMPLES, dtype=np.float32))[:, None]
    phases = time * np.asarray(FREQUENCIES, np.float32)[None, :]
    table = np.stack([np.cos(phases), np.sin(phases)], axis=2).reshape(SAMPLES, CH).astype(np.float32)
    hi = table.astype(jnp.bfloat16)
    eye = np.eye(8, dtype=np.float32)
    wide = [np.kron(x.astype(np.float32), eye) for x in (hi, hi)]
    return jnp.asarray(np.concatenate(wide, axis=1), BF16)


def sweep(idx, g, harm, elevation, depth, friction, mask, before, after, west, east, w):
    def whole(shape):
        return pl.BlockSpec(shape, lambda i, x: (0,) * len(shape))

    return pl.pallas_call(
        sweep_kernel,
        grid_spec=pltpu.PrefetchScalarGridSpec(
            num_scalar_prefetch=1,
            grid=(4,),
            in_specs=[
                whole((256, 1152)),
                whole((528, COLS + 128)),
                whole((CH, ROWS, COLS)),
                whole((ROWS, COLS)),
                whole((ROWS, COLS)),
                whole((ROWS, COLS)),
                whole((24, COLS)),
                whole((24, COLS)),
                whole((8, 1152)),
                whole((8, 1152)),
                whole((512, 256)),
            ],
            out_specs=[
                pl.BlockSpec((CH, 16, COLS), lambda i, x: (0, i, 0)),
                pl.BlockSpec(memory_space=pl.ANY),
                pl.BlockSpec((16, COLS), lambda i, x: (i, 0)),
            ],
            scratch_shapes=[
                pltpu.VMEM((CH, 80, COLS), F32),
                pltpu.VMEM((80, COLS), F32),
                pltpu.VMEM((80, COLS), F32),
                pltpu.VMEM((CH, 72, COLS), F32),
                pltpu.VMEM((CH, ROWS, COLS), F32),
                pltpu.VMEM((CH + 2, ROWS, 128), F32),
                pltpu.SemaphoreType.DMA((4,)),
            ],
        ),
        out_shape=[
            jax.ShapeDtypeStruct((CH, ROWS, COLS), F32),
            jax.ShapeDtypeStruct((CH, ROWS, COLS), F32),
            jax.ShapeDtypeStruct((ROWS, COLS), F32),
        ],
        compiler_params=params(),
        name="sweep",
    )(idx, g, harm, elevation, depth, friction, mask, before, after, west, east, w)


LAT = ("zh", "x", "c")
LON = ("y", "zl")


def shift(value, axes, size, step):
    return lax.ppermute(value, axes, [(i, (i + step) % size) for i in range(size)])


def shift_lat(value, step):
    return lax.ppermute(value, LAT, [(i, i + step) for i in range(32) if 0 <= i + step < 32])


def all_shifts(values, axis):
    return [shift(value, axis, 4, k + 1) for k, value in enumerate(values)]


def swap(x, axis):
    return lax.all_to_all(x, axis, 0, 0, tiled=True)


def on_device(elevation, depth, friction, land_mask, order_map, legendre, load):
    lat = lax.axis_index(LAT)
    lon = lax.axis_index(LON)
    core = lax.axis_index("c")
    x, z = lax.axis_index("x"), lax.axis_index("zh")
    idx = jnp.stack([lat, lon, core, x, z]).astype(jnp.int32)

    part, harm, half, first_row, last_row, ends = dft(
        idx, order_map[None, :], elevation, land_mask, depth, friction, legendre
    )
    received = swap(part.astype(jnp.float16), ("y", "zl", "c"))
    other = shift(half, "c", 2, 1)
    before = shift_lat(last_row, 1)
    after = shift_lat(first_row, -1)
    west = shift(ends, LON, 8, 1)
    east = shift(ends, LON, 8, -1)
    fourier = jnp.sum(received.reshape(8, 2, 16, 1024).astype(F32), axis=0) * (1.0 / PART_SCALE)
    own, *parts, mid, outer = analyse(idx, fourier, legendre, other, (before, after, west, east), BF16)
    prior = shift_lat(outer, 2)
    later = shift_lat(outer, -2)

    own, *parts = add_bands(idx, own, all_shifts(parts, "x"), BF16)
    total = own + sum(part.astype(F32) for part in all_shifts(parts, "zh"))
    scaled = (total * load[None, :]).astype(BF16)
    by_z = jnp.stack([scaled, *all_shifts([scaled] * 3, "zh")])
    spread = synthesise(
        idx, [by_z, *all_shifts([by_z] * 3, "x")], legendre, other, (mid, prior, later), BF16
    )
    g = swap(spread, ("y", "zl", "c"))
    new, sal, fnew = sweep(
        idx, g.reshape(256, 1152), harm, elevation, depth, friction, land_mask,
        before, after, west, east, sample_matrix(),
    )
    return new, sal, fnew


def solution(mesh):
    fine = Mesh(mesh.devices.reshape(4, 4, 2, 4, 2), ("zh", "x", "c", "y", "zl"))
    return jax.shard_map(
        on_device,
        mesh=fine,
        in_specs=(
            P(None, LAT, LON),
            P(LAT, LON),
            P(LAT, LON),
            P(LAT, LON),
            P(),
            P(LON, LAT, None),
            P(),
        ),
        out_specs=(P(None, LAT, LON), P(None, LAT, LON), P(LAT, LON)),
        check_vma=False,
    )
```

```python
import functools
import math

import jax
import jax.numpy as jnp
import numpy as np
from jax import lax
from jax.experimental import pallas as pl
from jax.experimental.pallas import tpu as pltpu
from jax.sharding import Mesh, PartitionSpec as P

SAMPLES = 64
FREQUENCIES = (1.0, 1.0347, 0.9582, 1.0379, 0.5018, 0.4651, 0.4986, 0.4482)
EQ_AMPS = (0.73, 0.34, 0.14, 0.09, 0.42, 0.3, 0.14, 0.06)
LAT_EDGE = 1.3614
RELAX_RATE = 0.1
BASE_FRICTION = 0.05
DRAG_COEFF = 0.5
SPEED_EPS = 0.001
STEP_TIME = 3.0
NLAT = 2048
NLON = 4096
LAT_STEP = 2.0 * LAT_EDGE / NLAT
ROWS = 64
COLS = 512
CH = 16
DEG = 2048
F32 = jnp.float32
BF16 = jnp.bfloat16
PART_SCALE = 512.0


def params(mib=24):
    return pltpu.CompilerParams(vmem_limit_bytes=mib * 1024 * 1024)


def unit_circle(k):
    k = k & (NLON - 1)
    quad = (k + 512) >> 10
    t = (k - (quad << 10)).astype(F32) * (2.0 * math.pi / NLON)
    q = quad & 3
    t2 = t * t
    s = t * (1.0 + t2 * (-1.0 / 6 + t2 * (1.0 / 120 + t2 * (-1.0 / 5040 + t2 * (1.0 / 362880)))))
    c = 1.0 + t2 * (-0.5 + t2 * (1.0 / 24 + t2 * (-1.0 / 720 + t2 * (1.0 / 40320))))
    swap = (q & 1) == 1
    cos = jnp.where(swap, s, c)
    sin = jnp.where(swap, c, s)
    cos = jnp.where((q == 1) | (q == 2), -cos, cos)
    sin = jnp.where(q >= 2, -sin, sin)
    return cos, sin


def split(x):
    hi = x.astype(BF16)
    lo = (x - hi.astype(F32)).astype(BF16)
    return hi, lo


NT = (((1,), (1,)), ((), ()))
TN = (((0,), (0,)), ((), ()))


def dft_kernel(
    idx, om_ref, elev_ref, mask_ref, depth_ref, fric_ref, leg_ref,
    part_ref, harm_ref, half_ref, first_ref, last_ref, cols_ref,
):
    i = pl.program_id(0)
    half_ref[...] = leg_ref[...]
    mask = mask_ref[...].astype(F32)
    @pl.when(i == 0)
    def _():
        diag = lax.broadcasted_iota(jnp.int32, (128, 128), 0) == lax.broadcasted_iota(jnp.int32, (128, 128), 1)
        orders = jnp.broadcast_to(om_ref[...].astype(F32), (128, 128))
        orders = jnp.sum(jnp.where(diag, orders, 0.0), axis=1, keepdims=True).astype(jnp.int32)
        lane = lax.broadcasted_iota(jnp.int32, (8, COLS + 128), 1)
        off = jnp.where(lane < COLS, lane, jnp.where(lane < COLS + 64, -1, COLS))
        col = idx[1] * COLS + off
        for g in range(16):
            m = orders[8 * g : 8 * g + 8, :]
            cos, sin = unit_circle(m * col)
            scale = jnp.where(m > 0, math.sqrt(2.0 / NLON), math.sqrt(1.0 / NLON)).astype(F32)
            hi, lo = split(jnp.concatenate([cos * scale, sin * scale], axis=0))
            harm_ref[16 * g : 16 * g + 16, :] = lo
            harm_ref[272 + 16 * g : 288 + 16 * g, :] = hi
        sub = lax.broadcasted_iota(jnp.int32, (16, COLS + 128), 0)
        lane = lax.broadcasted_iota(jnp.int32, (16, COLS + 128), 1)
        ends = ((sub == 0) & (lane == 0)) | ((sub == 1) & (lane == COLS - 1))
        harm_ref[256:272, :] = jnp.where(ends, 1.0, 0.0).astype(BF16)
        sea = depth_ref[...] * mask
        for r, x in ((16, sea), (17, fric_ref[...])):
            first_ref[r : r + 1, :] = x[:1]
            last_ref[r : r + 1, :] = x[ROWS - 1 :]
        first_ref[18:, :] = jnp.zeros((6, COLS), F32)
        last_ref[18:, :] = jnp.zeros((6, COLS), F32)
        pick = harm_ref[256:272, :COLS]
        hi, lo = split(jnp.concatenate([sea, fric_ref[...]], axis=0))
        edge = lax.dot_general(pick, hi, NT, preferred_element_type=F32)
        edge = edge + lax.dot_general(pick, lo, NT, preferred_element_type=F32)
        cols_ref[:, 1024:] = edge[:8]

    field = jnp.concatenate([elev_ref[c] * mask for c in range(8)], axis=0)
    hi, lo = split(field)
    both = lax.dot_general(harm_ref[:, :COLS], hi, NT, preferred_element_type=F32)
    small = lax.dot_general(harm_ref[256:, :COLS], lo, NT, preferred_element_type=F32)
    out = both[272:] + (both[:256] + small[16:])
    part_ref[...] = (out * PART_SCALE).reshape(16, 16, 512).astype(part_ref.dtype)
    for c in range(8):
        first_ref[pl.ds(8 * i + c, 1), :] = field[64 * c : 64 * c + 1]
        last_ref[pl.ds(8 * i + c, 1), :] = field[64 * c + 63 : 64 * c + 64]
    cols_ref[:, pl.ds(pl.multiple_of(512 * i, 512), 512)] = both[256:264] + small[:8]


def dft(idx, om, elevation, mask, depth, friction, legendre):
    def whole(shape):
        return pl.BlockSpec(shape, lambda i, x: (0,) * len(shape))

    return pl.pallas_call(
        dft_kernel,
        grid_spec=pltpu.PrefetchScalarGridSpec(
            num_scalar_prefetch=1,
            grid=(2,),
            in_specs=[
                whole((1, 128)),
                pl.BlockSpec((8, ROWS, COLS), lambda i, x: (i, 0, 0)),
                whole((ROWS, COLS)),
                whole((ROWS, COLS)),
                whole((ROWS, COLS)),
                pl.BlockSpec((4, ROWS, DEG), lambda i, x: (2 - 2 * x[2] + i, 0, 0)),
            ],
            out_specs=[
                pl.BlockSpec((16, 16, 512), lambda i, x: (0, 0, i)),
                whole((528, COLS + 128)),
                pl.BlockSpec((4, ROWS, DEG), lambda i, x: (i, 0, 0)),
                whole((24, COLS)),
                whole((24, COLS)),
                whole((8, 1152)),
            ],
        ),
        out_shape=[
            jax.ShapeDtypeStruct((16, 16, 1024), F32),
            jax.ShapeDtypeStruct((528, COLS + 128), BF16),
            jax.ShapeDtypeStruct((8, ROWS, DEG), BF16),
            jax.ShapeDtypeStruct((24, COLS), F32),
            jax.ShapeDtypeStruct((24, COLS), F32),
            jax.ShapeDtypeStruct((8, 1152), F32),
        ],
        compiler_params=params(60),
        name="dft",
    )(idx, om, elevation, mask, depth, friction, legendre)


def analyse_kernel(idx, r_ref, own_ref, rcv_ref, *rest):
    outs, (mid_ref, outer_ref, a_ref, e_ref) = rest[-8:-4], rest[-4:]

    @pl.when(pl.program_id(0) == 0)
    def _():
        me = idx[2]
        low = lax.broadcasted_iota(jnp.int32, (16, 128), 1) < 64
        for t in range(8):
            tiles = [r_ref[which, :, 128 * t : 128 * t + 128] for which in (me, 1 - me)]
            f0, f1 = tiles
            even = jnp.where(low, f0, pltpu.roll(f1, 64, 1))
            odd = jnp.where(low, pltpu.roll(f0, 64, 1), f1)
            for ch, val in ((2 * t, even), (2 * t + 1, odd)):
                for p in range(2):
                    a_ref[pl.ds(16 * p + ch, 8, stride=32), :] = val[8 * p : 8 * p + 8, :]

    i = pl.program_id(0)
    pair = (idx[3] + i) & 3
    for s in range(2):
        a = a_ref[pl.ds(pl.multiple_of(64 * pair, 64) + 32 * s, 32), :].astype(BF16)
        table = jnp.concatenate([own_ref[s], rcv_ref[s]], axis=0)
        sums = jnp.dot(a, table, preferred_element_type=F32)
        for k, out_ref in enumerate(outs):

            @pl.when(i == k)
            def _():
                out_ref[s] = sums.astype(out_ref.dtype)

        low = idx[2] == 0
        own_first, own_last = own_ref[s, :16].astype(F32)[:1], own_ref[s, ROWS - 16 :].astype(F32)[15:]
        rcv_first, rcv_last = rcv_ref[s, :16].astype(F32)[:1], rcv_ref[s, ROWS - 16 :].astype(F32)[15:]
        e_ref[pl.ds(2 * pair + s, 1), :] = jnp.where(low, rcv_first, own_first)
        e_ref[pl.ds(8 + 2 * pair + s, 1), :] = jnp.where(low, own_last, rcv_last)
        e_ref[pl.ds(16 + 2 * pair + s, 1), :] = jnp.where(low, own_first, rcv_first)
        e_ref[pl.ds(24 + 2 * pair + s, 1), :] = jnp.where(low, rcv_last, own_last)

    @pl.when(i == 3)
    def _():
        mid_ref[...] = e_ref[:16, :].astype(BF16)
        outer_ref[...] = e_ref[16:, :].astype(BF16)


def analyse(idx, received, legendre, other, after, dtype):
    whole = pl.BlockSpec((2, 32, DEG), lambda i, x: (0, 0, 0))
    return pl.pallas_call(
        analyse_kernel,
        grid_spec=pltpu.PrefetchScalarGridSpec(
            num_scalar_prefetch=1,
            grid=(4,),
            in_specs=[
                pl.BlockSpec((2, 16, 1024), lambda i, x: (0, 0, 0)),
                pl.BlockSpec((2, ROWS, DEG), lambda i, x: (4 * x[2] + ((x[3] + i) & 3), 0, 0)),
                pl.BlockSpec((2, ROWS, DEG), lambda i, x: ((x[3] + i) & 3, 0, 0)),
            ]
            + [pl.BlockSpec(memory_space=pl.ANY)] * len(after),
            out_specs=[
                whole,
                whole,
                whole,
                whole,
                pl.BlockSpec((16, DEG), lambda i, x: (0, 0)),
                pl.BlockSpec((16, DEG), lambda i, x: (0, 0)),
            ],
            scratch_shapes=[pltpu.VMEM((256, 128), F32), pltpu.VMEM((32, DEG), F32)],
        ),
        out_shape=[
            jax.ShapeDtypeStruct((2, 32, DEG), F32),
            jax.ShapeDtypeStruct((2, 32, DEG), dtype),
            jax.ShapeDtypeStruct((2, 32, DEG), dtype),
            jax.ShapeDtypeStruct((2, 32, DEG), dtype),
            jax.ShapeDtypeStruct((16, DEG), BF16),
            jax.ShapeDtypeStruct((16, DEG), BF16),
        ],
        compiler_params=params(),
        name="analyse",
    )(idx, received, legendre, other, *after)


def add_kernel(idx, own_ref, a_ref, b_ref, c_ref, *outs):
    for k, out_ref in enumerate(outs):
        z = (idx[4] + k) & 3
        total = own_ref[z] + a_ref[z].astype(F32) + b_ref[z].astype(F32) + c_ref[z].astype(F32)
        out_ref[...] = total.astype(out_ref.dtype)


def add_bands(idx, own, others, dtype):
    part = pl.BlockSpec((4, 16, DEG), lambda i, x: (0, 0, 0))
    return pl.pallas_call(
        add_kernel,
        grid_spec=pltpu.PrefetchScalarGridSpec(
            num_scalar_prefetch=1,
            grid=(1,),
            in_specs=[part] * 4,
            out_specs=[pl.BlockSpec((16, DEG), lambda i, x: (0, 0))] * 4,
        ),
        out_shape=[jax.ShapeDtypeStruct((16, DEG), t) for t in (F32, dtype, dtype, dtype)],
        compiler_params=params(),
        name="add_bands",
    )(idx, own.reshape(4, 16, DEG), *[x.reshape(4, 16, DEG) for x in others])


def synth_kernel(idx, w0_ref, w1_ref, w2_ref, w3_ref, own_ref, rcv_ref, mid_ref, prev_ref, next_ref, out_ref, sc_ref, t_ref, u_ref):
    edges = jnp.concatenate([mid_ref[...], prev_ref[...], next_ref[...]], axis=0)
    i = pl.program_id(0)
    pair = (idx[3] - i) & 3
    for k, w_ref in enumerate((w0_ref, w1_ref, w2_ref, w3_ref)):

        @pl.when(i == k)
        def _():
            for z in range(4):
                sc_ref[16 * z : 16 * z + 16, :] = w_ref[(idx[4] - z) & 3]

    for s in range(2):
        table = jnp.concatenate([own_ref[s], rcv_ref[s]], axis=0)
        row = pl.multiple_of(64 * pair, 64) + 32 * s
        scaled = sc_ref[32 * s : 32 * s + 32, :]
        t_ref[pl.ds(row, 32), :] = lax.dot_general(scaled, table, NT, preferred_element_type=F32)
        u_ref[2 * pair + s, :, :32] = lax.dot_general(edges, scaled, NT, preferred_element_type=F32)

    @pl.when(i == 3)
    def _():
        me = idx[2]
        lane = lax.broadcasted_iota(jnp.int32, (8, 128), 1)
        sub = lax.broadcasted_iota(jnp.int32, (8, 128), 0)
        low = lane < 64
        for t in range(8):
            own, oth = [], []
            for p in range(2):
                v0 = t_ref[pl.ds(16 * p + 2 * t, 8, stride=32), :]
                v1 = t_ref[pl.ds(16 * p + 2 * t + 1, 8, stride=32), :]
                own.append(jnp.where(low, v0, pltpu.roll(v1, 64, 1)))
                oth.append(jnp.where(low, pltpu.roll(v0, 64, 1), v1))
            own = jnp.concatenate(own, axis=0).astype(out_ref.dtype)
            oth = jnp.concatenate(oth, axis=0).astype(out_ref.dtype)
            for d in range(8):
                out_ref[2 * d + me, :, 128 * t : 128 * t + 128] = own
                out_ref[2 * d + 1 - me, :, 128 * t : 128 * t + 128] = oth
        for half in range(2):
            sides = []
            for side in range(2):
                g = 8 * ((3, 0), (1, 4))[half][side]
                v = jnp.zeros((8, 128), F32)
                for s in range(8):
                    v = jnp.where(sub == s, u_ref[s, g : g + 8, :], v)
                sides.append(v)
            top, bottom = sides
            rows = [
                jnp.where(lane < 16, top, pltpu.roll(bottom, 16, 1)),
                jnp.where(lane < 16, pltpu.roll(top, 112, 1), bottom),
            ]
            rows = [jnp.where(lane < 32, x, 0.0) for x in rows]
            edge = jnp.concatenate(rows, axis=0).astype(out_ref.dtype)
            for d in range(8):
                out_ref[2 * d + half, :, 1024:] = edge


def synthesise(idx, parts, legendre, other, edges, dtype):
    def whole(shape):
        return pl.BlockSpec(shape, lambda i, x: (0,) * len(shape))

    return pl.pallas_call(
        synth_kernel,
        grid_spec=pltpu.PrefetchScalarGridSpec(
            num_scalar_prefetch=1,
            grid=(4,),
            in_specs=[whole((4, 16, DEG))] * 4
            + [
                pl.BlockSpec((2, ROWS, DEG), lambda i, x: (4 * x[2] + ((x[3] - i) & 3), 0, 0)),
                pl.BlockSpec((2, ROWS, DEG), lambda i, x: ((x[3] - i) & 3, 0, 0)),
            ]
            + [whole((16, DEG))] * 3,
            out_specs=whole((16, 16, 1152)),
            scratch_shapes=[
                pltpu.VMEM((64, DEG), BF16),
                pltpu.VMEM((256, 128), F32),
                pltpu.VMEM((8, 48, 128), F32),
            ],
        ),
        out_shape=jax.ShapeDtypeStruct((16, 16, 1152), dtype),
        compiler_params=params(),
        name="synthesise",
    )(idx, *parts, legendre, other, *edges)


def lat_of(row):
    return -LAT_EDGE + row * LAT_STEP


def sweep_kernel(
    idx, g_ref, harm_ref, elev_ref, depth_ref, fric_ref, mask_ref, before_ref, after_ref, west_ref, east_ref, w_ref,
    new_ref, sal_ref, fnew_ref, spad, dpad, fpad, nf, salbuf, lonh_all, sem,
):
    b = pl.program_id(0)
    lat0 = idx[0] * ROWS

    def send(c):
        part = pl.ds(4 * c, 4)
        return pltpu.make_async_copy(salbuf.at[part], sal_ref.at[part], sem.at[c])

    @pl.when(b == 0)
    def _():
        lane = lax.broadcasted_iota(jnp.int32, (8, COLS), 1)
        col = idx[1] * COLS + lane
        c1, s1 = unit_circle(col)
        c2, s2 = unit_circle(2 * col)
        waves = (c2[:1], s2[:1], c1[:1], s1[:1])

        def shapes(first, count):
            row = first.astype(F32) + lax.broadcasted_iota(jnp.int32, (count, 128), 0).astype(F32)
            phi = lat_of(row + 0.5)
            cosphi = jnp.cos(phi)
            return jnp.tile(cosphi * cosphi, (1, 4)), jnp.tile(jnp.sin(2.0 * phi), (1, 4))

        sq, s2phi = shapes(lat0, ROWS)
        up_sq, up_s2 = shapes(lat0 - 1, 8)
        dn_sq, dn_s2 = shapes(lat0 + ROWS, 8)

        def invert(cols):
            part = g_ref[:, cols]
            hi = lax.dot_general(part, harm_ref[272:, :], TN, preferred_element_type=F32)
            lo = lax.dot_general(part, harm_ref[:256, :], TN, preferred_element_type=F32)
            return hi + lo

        sub = lax.broadcasted_iota(jnp.int32, (32, 128), 0) & 15
        lane = lax.broadcasted_iota(jnp.int32, (32, 128), 1)
        place = ((sub == 1) & (lane < 64)) | ((sub == 8) & (lane >= 64))
        place = jnp.where(place, 1.0, 0.0).astype(BF16)
        hi, lo = split(jnp.concatenate([west_ref[...], east_ref[...]], axis=0))
        beside = lax.dot_general(jnp.concatenate([hi, lo], axis=0), place, TN, preferred_element_type=F32)
        for ch in range(18):
            lonh_all[ch] = beside[64 * ch : 64 * ch + 64]
        edge = invert(slice(1024, 1152))
        for ch in range(CH):
            if ch % 4 == 0:
                quarter = invert(slice(64 * ch, 64 * ch + 256))
                for c in range(4):
                    salbuf[ch + c] = quarter[64 * c : 64 * c + 64, :COLS]
                    lonh_all[ch + c] = lonh_all[ch + c] - quarter[64 * c : 64 * c + 64, COLS:]
                send(ch // 4).start()
            k = ch // 2
            wave = waves[(0 if k < 4 else 2) + ch % 2]
            eq = EQ_AMPS[k] * (sq if k < 4 else s2phi) * wave
            spad[ch, 8 : 8 + ROWS, :] = elev_ref[ch] - eq - salbuf[ch]
            up = EQ_AMPS[k] * (up_sq if k < 4 else up_s2)[:1] * wave
            dn = EQ_AMPS[k] * (dn_sq if k < 4 else dn_s2)[:1] * wave
            spad[ch, 7:8, :] = before_ref[ch : ch + 1, :] - up - edge[ch : ch + 1, :COLS]
            spad[ch, 8 + ROWS : 9 + ROWS, :] = after_ref[ch : ch + 1, :] - dn - edge[16 + ch : 17 + ch, :COLS]
        dpad[8 : 8 + ROWS, :] = depth_ref[...] * mask_ref[...].astype(F32)
        fpad[8 : 8 + ROWS, :] = fric_ref[...]
        top = jnp.where(idx[0] == 0, 0.0, 1.0)
        bottom = jnp.where(idx[0] == 31, 0.0, 1.0)
        dpad[7:8, :] = before_ref[16:17, :] * top
        dpad[8 + ROWS : 9 + ROWS, :] = after_ref[16:17, :] * bottom
        fpad[7:8, :] = before_ref[17:18, :]
        fpad[8 + ROWS : 9 + ROWS, :] = after_ref[17:18, :]

        for blk in range(9):
            lo = 8 * blk
            row = (lat0 + lo).astype(F32) + lax.broadcasted_iota(jnp.int32, (8, 128), 0).astype(F32)
            cosf = jnp.tile(jnp.cos(lat_of(row)), (1, 4))
            hh = dpad[8 + lo : 16 + lo, :] * dpad[7 + lo : 15 + lo, :]
            h = jnp.sqrt(hh)
            r = 0.5 * (fpad[8 + lo : 16 + lo, :] + fpad[7 + lo : 15 + lo, :])
            for k in range(8):
                om = FREQUENCIES[k]
                inv = -hh / (r * r + (om * om) * hh)
                rc = inv * r * cosf
                ic = inv * h * om * cosf
                dr = spad[2 * k, 8 + lo : 16 + lo, :] - spad[2 * k, 7 + lo : 15 + lo, :]
                di = spad[2 * k + 1, 8 + lo : 16 + lo, :] - spad[2 * k + 1, 7 + lo : 15 + lo, :]
                nf[2 * k, lo : lo + 8, :] = rc * dr - ic * di
                nf[2 * k + 1, lo : lo + 8, :] = rc * di + ic * dr

    def sweep_rows(sub_block):
        out = slice(8 * sub_block, 8 * sub_block + 8)
        base = pl.multiple_of(8 * (2 * b + sub_block), 8)
        own = pl.ds(base + 8, 8)
        row = (lat0 + base).astype(F32) + lax.broadcasted_iota(jnp.int32, (8, 128), 0).astype(F32)
        phi = lat_of(row + 0.5)
        rcos1 = 1.0 / jnp.cos(phi)
        rcos = jnp.tile(rcos1, (1, 4))
        lane = lax.broadcasted_iota(jnp.int32, (8, COLS), 1)
        last = lane == COLS - 1
        first = lane == 0
        tile_lane = lax.broadcasted_iota(jnp.int32, (8, 128), 1)
        col = idx[1] * COLS + jnp.where(tile_lane < 64, -1, COLS)
        c1, s1 = unit_circle(col)
        c2, s2 = unit_circle(2 * col)
        waves = (c2, s2, c1, s1)
        cosphi = jnp.cos(phi)
        sq, s2phi = cosphi * cosphi, jnp.sin(2.0 * phi)

        def east_of(x, halo):
            wide = jnp.tile(halo, (1, 4))
            return jnp.where(last, wide, pltpu.roll(x, COLS - 1, 1))

        d = dpad[own, :]
        f = fpad[own, :]
        dh = lonh_all[16, pl.ds(base, 8), :]
        fh = lonh_all[17, pl.ds(base, 8), :]
        hh = d * east_of(d, dh)
        h = jnp.sqrt(hh)
        r = 0.5 * (f + east_of(f, fh))
        hhw = d[:, :128] * dh
        hw = jnp.sqrt(hhw)
        rw = 0.5 * (f[:, :128] + fh)
        mask = mask_ref[pl.ds(base, 8), :].astype(F32)
        ecell, ncell = [], []
        for k in range(8):
            om = FREQUENCIES[k]
            inv = -hh / (r * r + (om * om) * hh)
            rc = inv * r * rcos
            ic = inv * h * om * rcos
            invw = -hhw / (rw * rw + (om * om) * hhw)
            rcw = invw * rw * rcos1
            icw = invw * hw * om * rcos1
            diffs, wdiffs = [], []
            for ch in (2 * k, 2 * k + 1):
                s = spad[ch, own, :]
                eq = EQ_AMPS[k] * (sq if k < 4 else s2phi) * waves[(0 if k < 4 else 2) + ch % 2]
                sh = lonh_all[ch, pl.ds(base, 8), :] - eq
                diffs.append(east_of(s, sh) - s)
                wdiffs.append(s[:, :128] - sh)
            flux = (rc * diffs[0] - ic * diffs[1], rc * diffs[1] + ic * diffs[0])
            fluxw = (rcw * wdiffs[0] - icw * wdiffs[1], rcw * wdiffs[1] + icw * wdiffs[0])
            div = []
            for p in range(2):
                ch = 2 * k + p
                west = jnp.where(first, jnp.tile(fluxw[p], (1, 4)), pltpu.roll(flux[p], 1, 1))
                south = nf[ch, pl.ds(base, 8), :]
                below = nf[ch, pl.ds(base + 8, 8), :]
                sub = lax.broadcasted_iota(jnp.int32, (8, COLS), 0)
                north = pltpu.roll(jnp.where(sub == 0, below, south), 7, 0)
                div.append((flux[p] - west + (north - south)) * rcos)
                ecell.append(0.5 * (flux[p] + west))
                ncell.append(0.5 * (north + south))
            cr = elev_ref[2 * k, pl.ds(base, 8), :]
            ci = elev_ref[2 * k + 1, pl.ds(base, 8), :]
            new_ref[2 * k, out] = (cr - RELAX_RATE * (div[0] + om * ci)) * mask
            new_ref[2 * k + 1, out] = (ci - RELAX_RATE * (div[1] - om * cr)) * mask

        def stacked(parts):
            hi, lo = split(jnp.concatenate(parts, axis=0))
            return jnp.concatenate([hi, lo], axis=0)

        xe, xn = stacked(ecell), stacked(ncell)
        total = jnp.zeros((8, COLS), F32)
        for q in range(4):
            w = w_ref[128 * q : 128 * q + 128, :]
            u = jnp.dot(w, xe, preferred_element_type=F32)
            v = jnp.dot(w, xn, preferred_element_type=F32)
            x = u * u + v * v + SPEED_EPS * SPEED_EPS
            speed = x * lax.rsqrt(x)
            for s in range(16):
                total = total + speed[8 * s : 8 * s + 8, :]
        fnew_ref[out, :] = BASE_FRICTION + DRAG_COEFF * total / SAMPLES

    for sub_block in range(2):
        sweep_rows(sub_block)

    @pl.when(b == 3)
    def _():
        for c in range(4):
            send(c).wait()


def sample_matrix():
    time = (STEP_TIME * np.arange(SAMPLES, dtype=np.float32))[:, None]
    phases = time * np.asarray(FREQUENCIES, np.float32)[None, :]
    table = np.stack([np.cos(phases), np.sin(phases)], axis=2).reshape(SAMPLES, CH).astype(np.float32)
    hi = table.astype(jnp.bfloat16)
    eye = np.eye(8, dtype=np.float32)
    wide = [np.kron(x.astype(np.float32), eye) for x in (hi, hi)]
    return jnp.asarray(np.concatenate(wide, axis=1), BF16)


def sweep(idx, g, harm, elevation, depth, friction, mask, before, after, west, east, w):
    def whole(shape):
        return pl.BlockSpec(shape, lambda i, x: (0,) * len(shape))

    return pl.pallas_call(
        sweep_kernel,
        grid_spec=pltpu.PrefetchScalarGridSpec(
            num_scalar_prefetch=1,
            grid=(4,),
            in_specs=[
                whole((256, 1152)),
                whole((528, COLS + 128)),
                whole((CH, ROWS, COLS)),
                whole((ROWS, COLS)),
                whole((ROWS, COLS)),
                whole((ROWS, COLS)),
                whole((24, COLS)),
                whole((24, COLS)),
                whole((8, 1152)),
                whole((8, 1152)),
                whole((512, 256)),
            ],
            out_specs=[
                pl.BlockSpec((CH, 16, COLS), lambda i, x: (0, i, 0)),
                pl.BlockSpec(memory_space=pl.ANY),
                pl.BlockSpec((16, COLS), lambda i, x: (i, 0)),
            ],
            scratch_shapes=[
                pltpu.VMEM((CH, 80, COLS), F32),
                pltpu.VMEM((80, COLS), F32),
                pltpu.VMEM((80, COLS), F32),
                pltpu.VMEM((CH, 72, COLS), F32),
                pltpu.VMEM((CH, ROWS, COLS), F32),
                pltpu.VMEM((CH + 2, ROWS, 128), F32),
                pltpu.SemaphoreType.DMA((4,)),
            ],
        ),
        out_shape=[
            jax.ShapeDtypeStruct((CH, ROWS, COLS), F32),
            jax.ShapeDtypeStruct((CH, ROWS, COLS), F32),
            jax.ShapeDtypeStruct((ROWS, COLS), F32),
        ],
        compiler_params=params(),
        name="sweep",
    )(idx, g, harm, elevation, depth, friction, mask, before, after, west, east, w)


LAT = ("zh", "x", "c")
LON = ("y", "zl")


def shift(value, axes, size, step):
    return lax.ppermute(value, axes, [(i, (i + step) % size) for i in range(size)])


def shift_lat(value, step):
    return lax.ppermute(value, LAT, [(i, i + step) for i in range(32) if 0 <= i + step < 32])


def all_shifts(values, axis):
    return [shift(value, axis, 4, k + 1) for k, value in enumerate(values)]


def swap(x, axis):
    return lax.all_to_all(x, axis, 0, 0, tiled=True)


def on_device(elevation, depth, friction, land_mask, order_map, legendre, load):
    lat = lax.axis_index(LAT)
    lon = lax.axis_index(LON)
    core = lax.axis_index("c")
    x, z = lax.axis_index("x"), lax.axis_index("zh")
    idx = jnp.stack([lat, lon, core, x, z]).astype(jnp.int32)

    part, harm, half, first_row, last_row, ends = dft(
        idx, order_map[None, :], elevation, land_mask, depth, friction, legendre
    )
    received = swap(part.astype(jnp.float16), ("y", "zl", "c"))
    other = shift(half, "c", 2, 1)
    before = shift_lat(last_row, 1)
    after = shift_lat(first_row, -1)
    west = shift(ends, LON, 8, 1)
    east = shift(ends, LON, 8, -1)
    fourier = jnp.sum(received.reshape(8, 2, 16, 1024).astype(F32), axis=0) * (1.0 / PART_SCALE)
    own, *parts, mid, outer = analyse(idx, fourier, legendre, other, (before, after, west, east), BF16)
    prior = shift_lat(outer, 2)
    later = shift_lat(outer, -2)

    own, *parts = add_bands(idx, own, all_shifts(parts, "x"), BF16)
    total = own + sum(part.astype(F32) for part in all_shifts(parts, "zh"))
    scaled = (total * load[None, :]).astype(BF16)
    by_z = jnp.stack([scaled, *all_shifts([scaled] * 3, "zh")])
    spread = synthesise(
        idx, [by_z, *all_shifts([by_z] * 3, "x")], legendre, other, (mid, prior, later), BF16
    )
    g = swap(spread, ("y", "zl", "c"))
    new, sal, fnew = sweep(
        idx, g.reshape(256, 1152), harm, elevation, depth, friction, land_mask,
        before, after, west, east, sample_matrix(),
    )
    return new, sal, fnew


def solution(mesh):
    fine = Mesh(mesh.devices.reshape(4, 4, 2, 4, 2), ("zh", "x", "c", "y", "zl"))
    return jax.shard_map(
        on_device,
        mesh=fine,
        in_specs=(
            P(None, LAT, LON),
            P(LAT, LON),
            P(LAT, LON),
            P(LAT, LON),
            P(),
            P(LON, LAT, None),
            P(),
        ),
        out_specs=(P(None, LAT, LON), P(None, LAT, LON), P(LAT, LON)),
        check_vma=False,
    )
```
